32 devices in a mesh: key: 8 (over z, x), lvl: 4 (over y, core).
Axes of the slice: x: 2, y: 2, z: 4, core: 2. Of those that a mesh axis runs over, the one named last changes fastest.
Arguments:
- multipoles: bfloat16 [1024, 4096], P(('key', 'lvl')), may hold values from -6 to 6
- operators: bfloat16 [189, 64, 64], replicated, may hold values from -0.0546875 to 0.0546875
- pair_source: int32 [1024, 189], P(('key', 'lvl')), may hold values from 0 to 1087, as said below
- pair_offset: int32 [1024, 189], P(('key', 'lvl')), may hold values from 0 to 188, each once within a row
- live_pairs: int32 [1024], P(('key', 'lvl')), may hold values from 1 to 189
- send_lists: int32 [32, 32, 2], replicated, may hold values from 0 to 1023, as said below
- occupied: int32 [1024, 64], P(('key', 'lvl')), may hold values 0 or 1
Outputs:
- locals_out: float32 [1024, 4096], P(('key', 'lvl'))
The draws below stay inside these ranges and needn't reach their ends.
Inputs may be any that keep to these rules, and one draw needn't show every extreme that they name: `pair_source`: batch b belongs to device b // 32 (device index over key+lvl, key slowest). A value below 1024 is a batch of device j - 1, j or j + 1 for a target on device j. send_lists[i, j, k] is a batch owned by device i.
All inputs are finite; a program needn't handle non-finite values. No bound on the sum of `occupied` on one device may be relied on, other than what follows from the above.
Results may differ from the reference program's by a relative error of at most 0.0003.
Values may be sent and summed in bfloat16 or wider, within the bound.
No kernel may reach another device: no remote copies, remote signals or barrier semaphores. Data moves between devices by JAX's collectives and lax.ppermute only.
A program may use at most 64 MiB of HBM per device.

```python
import jax
import jax.numpy as jnp
from jax import lax

P_SIZE = 64
CB = 64
LIST = 189
BD = 32
CAP = 2
NB = 1024
DEVICES = 32


def draw_send_lists(key, part):
    key = jax.random.fold_in(key, 11)
    owners = jnp.arange(DEVICES, dtype=jnp.int32)[:, None, None] * BD
    tables = jax.random.randint(key, (DEVICES, DEVICES, CAP), 0, BD, dtype=jnp.int32) + owners
    tables = tables.at[DEVICES - 1, 0, 0].set(NB - 1)
    tables = tables.at[0, 0, 0].set(0)
    return tables.astype(jnp.int32)


def draw_pair_source(key, part):
    key = jax.random.fold_in(key, 3)
    first, second, third, fourth = jax.random.split(key, 4)
    target = jnp.arange(NB, dtype=jnp.int32)[:, None]
    owner = target // BD
    lower = jnp.maximum(0, (owner - 1) * BD)
    upper = jnp.minimum(NB - 1, (owner + 2) * BD - 1)
    jitter = jax.random.randint(first, (NB, LIST), -BD, BD + 1, dtype=jnp.int32)
    near = jnp.clip(target + jitter, lower, upper)
    peer = (owner + 1 + jax.random.randint(second, (NB, LIST), 0, DEVICES - 1, dtype=jnp.int32)) % DEVICES
    slot = jax.random.randint(third, (NB, LIST), 0, CAP, dtype=jnp.int32)
    far = NB + peer * CAP + slot
    pick = jax.random.randint(fourth, (NB, LIST), 0, 8, dtype=jnp.int32) == 0
    return jnp.where(pick, far, near).astype(jnp.int32)


def draw_live_pairs(key, part):
    key = jax.random.fold_in(key, 5)
    first, second = jax.random.split(key)
    limit = 48 + jax.random.randint(first, (DEVICES,), 0, LIST - 47, dtype=jnp.int32)
    limit_rows = jnp.repeat(limit, BD)
    raw = jax.random.randint(second, (NB,), 0, 1 << 20, dtype=jnp.int32)
    counts = 1 + raw % limit_rows
    return counts.at[0].set(LIST).astype(jnp.int32)


def with_ends(result, key, low, high):
    spot = [jax.random.randint(jax.random.fold_in(key, axis), (), 0, length) for axis, length in enumerate(result.shape)]
    main_axis = result.shape.index(max(result.shape))
    neighbour = spot[:main_axis] + [(spot[main_axis] + 1) % result.shape[main_axis]] + spot[main_axis + 1:]
    return result.at[tuple(spot)].set(low).at[tuple(neighbour)].set(high)


def block_scale(own_key, extent, pieces, low, largest):
    gain, own = 1.0, jax.random.fold_in(own_key, 6)
    for dim, parts in pieces:
        heights = jnp.exp(jax.random.uniform(jax.random.fold_in(own, dim), (parts,), jnp.float32, low / len(pieces), largest / len(pieces)))
        gain = gain * jnp.repeat(heights, extent[dim] // parts).reshape([-1 if axis == dim else 1 for axis in range(len(extent))])
    return gain


def gaussian(key, extent, width, bound, pieces=(), held_as=jnp.bfloat16):
    entries = jax.random.normal(key, extent, jnp.float32) * width
    if len(pieces) > 0:
        entries = block_scale(key, extent, pieces, -0.22, 0.18) * entries
    return jnp.clip(entries, min=-bound, max=bound).astype(held_as)


def setup_inputs(seed: int = 0) -> dict:
    splits = jax.random.split(jax.random.key(seed), 8)
    multipoles = gaussian(splits[0], (NB, P_SIZE * CB), 1.0, 6.0, ((0, 32),))
    operators = gaussian(splits[1], (LIST, P_SIZE, P_SIZE), (LIST * P_SIZE) ** -0.5, 0.0546875)
    pair_source = draw_pair_source(jax.random.fold_in(splits[7], 71), 0)
    pair_offset = jax.vmap(lambda own: jax.random.permutation(own, LIST))(jax.random.split(splits[3], NB)).reshape((NB, LIST)).astype(jnp.int32)
    live_pairs = draw_live_pairs(jax.random.fold_in(splits[7], 71), 0)
    send_lists = draw_send_lists(jax.random.fold_in(splits[7], 71), 0)
    occupied = with_ends((jax.random.randint(splits[6], (NB, CB), 0, 4) < 3).astype(jnp.int32), jax.random.fold_in(splits[6], 1), 0, 1)
    return dict(multipoles=multipoles, operators=operators, pair_source=pair_source, pair_offset=pair_offset, live_pairs=live_pairs, send_lists=send_lists, occupied=occupied)


def reference(multipoles, operators, pair_source, pair_offset, live_pairs, send_lists, occupied):
    span = 7
    target_dev = (jnp.arange(NB, dtype=jnp.int32) // BD)[:, None]
    code = jnp.maximum(pair_source - NB, 0)
    peer = code // CAP
    slot = code % CAP
    remote = send_lists[peer, jnp.broadcast_to(target_dev, pair_source.shape), slot]
    resolved = jnp.where(pair_source < NB, pair_source, remote).astype(jnp.int32)
    order = jnp.argsort(pair_offset, axis=1).astype(jnp.int32)
    by_offset = jnp.take_along_axis(resolved, order, axis=1)
    alive = order < live_pairs[:, None]
    index = jnp.where(alive, by_offset, NB).astype(jnp.int32)
    padded = jnp.concatenate([multipoles, jnp.zeros((1, P_SIZE * CB), jnp.bfloat16)], axis=0).reshape(NB + 1, CB, P_SIZE)

    def step(total, group):
        picked = lax.dynamic_slice_in_dim(index, group * span, span, 1)
        sources = padded[picked].astype(jnp.float32)
        mats = lax.dynamic_slice_in_dim(operators, group * span, span, 0).astype(jnp.float32)
        return total + jnp.einsum("gpq,tgcq->tcp", mats, sources), None

    start = jnp.zeros((NB, CB, P_SIZE), jnp.float32)
    total, unused = lax.scan(step, start, jnp.arange(LIST // span, dtype=jnp.int32))
    total = total * occupied[:, :, None].astype(jnp.float32)
    return total.reshape(NB, CB * P_SIZE)
```

```python
import functools

import jax
import jax.numpy as jnp
from jax import lax
from jax.experimental import pallas as pl
from jax.experimental.pallas import tpu as pltpu
from jax.sharding import PartitionSpec as P

F32 = jnp.float32
BF16 = jnp.bfloat16
I32 = jnp.int32
VMEM = pl.BlockSpec(memory_space=pltpu.VMEM)
SMEM = pl.BlockSpec(memory_space=pltpu.SMEM)
GROUP = 8
ITEMS = 4
LANES = 128


def params(mib):
    return pltpu.CompilerParams(vmem_limit_bytes=mib << 20)


def padded(n, m):
    return -(-n // m) * m


def pack_kernel(ids, m, own, outgoing, scr):
    batches, pairs = own.shape[0], own.shape[1]
    for i in range(pairs):
        for h in range(0, batches, 16):
            x = m[h : h + 16, i * LANES : (i + 1) * LANES].astype(F32)
            scr[pl.ds(h * pairs + i, 16, stride=pairs), :] = x
    for b in range(batches):
        own[b] = scr[b * pairs : (b + 1) * pairs, :].astype(BF16)

    def send(n, _):
        outgoing[n] = own[ids[n]]
        return 0

    lax.fori_loop(0, outgoing.shape[0], send, 0, unroll=8)


def table_kernel(total_batches, base, src, off, live, near_tbl, far_slot, far_off, far_items):
    rows, lst = src.shape
    wide = near_tbl.shape[1]
    s = src[...]
    o = off[...]
    col = lax.broadcasted_iota(I32, (rows, lst), 1)
    alive = col < live[...]
    far = s >= total_batches
    near_val = jnp.where(alive & jnp.logical_not(far), s - base[0] + 1, 0)
    far_live = alive & far
    far_val = jnp.where(far_live, s - total_batches + 1, 0)
    one = jnp.where(far_live, 1.0, 0.0)
    before = lax.broadcasted_iota(I32, (lst, lst), 0) < lax.broadcasted_iota(I32, (lst, lst), 1)
    rank = jnp.dot(one.astype(BF16), jnp.where(before, 1.0, 0.0).astype(BF16), preferred_element_type=F32)
    pos = jnp.where(far_live, rank.astype(I32), wide)
    count = jnp.sum(one, axis=1, keepdims=True).astype(I32)
    items = jnp.maximum((count + (GROUP - 1)) // GROUP, 1)
    far_items[...] = jnp.ones_like(far_items)
    far_items[0:rows, :] = jnp.broadcast_to(items, (rows, LANES))
    near_b = near_val.astype(F32).astype(BF16)
    far_b = jnp.concatenate([far_val & 127, far_val >> 7, o], axis=0).astype(F32).astype(BF16)
    want = lax.broadcasted_iota(I32, (wide, lst), 0)
    nt = (((1,), (1,)), ((), ()))
    far_slot[...] = jnp.zeros_like(far_slot)
    far_off[...] = jnp.zeros_like(far_off)
    for t in range(rows):
        hot = jnp.where(want == o[t : t + 1, :], 1.0, 0.0).astype(BF16)
        got = lax.dot_general(near_b, hot, nt, preferred_element_type=F32)
        near_tbl[t : t + 1, :] = got[t : t + 1, :].astype(I32)
        hot = jnp.where(want == pos[t : t + 1, :], 1.0, 0.0).astype(BF16)
        got = lax.dot_general(far_b, hot, nt, preferred_element_type=F32).astype(I32)
        far_slot[t : t + 1, :] = got[t : t + 1, :] + 128 * got[rows + t : rows + t + 1, :]
        far_off[t : t + 1, :] = got[2 * rows + t : 2 * rows + t + 1, :]


def near_kernel(tbl, before, own, after, ops, acc, pool):
    batches = own.shape[0]
    last = ops.shape[0] - 1
    zero = jnp.zeros(pool.shape[1:], BF16)
    pool[0] = zero
    for n, part in enumerate((before, own, after)):
        for b in range(batches):
            pool[1 + n * batches + b] = part[b]
    acc[...] = jnp.zeros_like(acc)
    blank = jnp.zeros(ops.shape[1:], BF16)

    def group(g, _):
        blocks = []
        for h in range(GROUP):
            op = ops[jnp.minimum(g * GROUP + h, last)]
            blocks.append(jnp.concatenate([op, blank], axis=1))
            blocks.append(jnp.concatenate([blank, op], axis=1))
        w = jnp.concatenate(blocks, axis=0)
        rows = []
        for t in range(batches):
            rows.append(jnp.concatenate([pool[tbl[t, g * GROUP + h]] for h in range(GROUP)], axis=1))
        x = jnp.concatenate(rows, axis=0)
        acc[...] += jnp.dot(x, w, preferred_element_type=F32).reshape(acc.shape)
        return 0

    lax.fori_loop(0, tbl.shape[1] // GROUP, group, 0)


def far_kernel(slots, offs, items, arrived, ops, near, occ, out, pool, rolled, acc):
    batches, pairs = near.shape[0], near.shape[1]
    half = ops.shape[2]
    zero = jnp.zeros(pool.shape[1:], BF16)
    pool[0] = zero
    rolled[0] = zero

    def fill(n, _):
        x = arrived[n]
        pool[n + 1] = x
        rolled[n + 1] = jnp.concatenate([x[:, half:], x[:, :half]], axis=1)
        return 0

    lax.fori_loop(0, arrived.shape[0], fill, 0, unroll=8)
    acc[0 : batches * pairs, :] = near[...].reshape(batches * pairs, LANES)
    acc[batches * pairs :, :] = jnp.zeros((pairs, LANES), F32)
    low = lax.broadcasted_iota(I32, (pairs, LANES), 1) < half
    total = lax.fori_loop(0, batches, lambda t, n: n + items[t, 0], 0)

    def step(i, place):
        t, g = place
        found = []
        for u in range(ITEMS):
            xs, ws = [], []
            for h in range(0, GROUP, 2):
                e = g * GROUP + h
                a, b = slots[t, e], slots[t, e + 1]
                even = jnp.where(low, pool[a], rolled[b])
                odd = jnp.where(low, rolled[a], pool[b])
                xs.append(jnp.concatenate([even, odd], axis=0))
                ws += [ops[offs[t, e]], ops[offs[t, e + 1]]]
            r = jnp.dot(jnp.concatenate(xs, axis=1), jnp.concatenate(ws, axis=0), preferred_element_type=F32)
            found.append((t, jnp.concatenate([r[:pairs], r[pairs:]], axis=1)))
            end = g + 1 >= items[t, 0]
            t = jnp.where(end, jnp.minimum(t + 1, batches), t)
            g = jnp.where(end, 0, g + 1)
        for at, r in found:
            acc[pl.ds(pl.multiple_of(at * pairs, pairs), pairs), :] += r
        return t, g

    lax.fori_loop(0, (total + (ITEMS - 1)) // ITEMS, step, (jnp.int32(0), jnp.int32(0)))
    for i in range(pairs):
        cols = slice(i * LANES, (i + 1) * LANES)
        out[:, cols] = acc[pl.ds(i, batches, stride=pairs), :] * occ[:, cols]


def local(multipoles, operators, pair_source, pair_offset, live_pairs, send_lists, occupied):
    axes = ("key", "lvl")
    batches, width = multipoles.shape
    offsets, coeffs = operators.shape[0], operators.shape[1]
    devices = lax.axis_size(axes)
    slots = send_lists.shape[2]
    me = lax.axis_index(axes)
    pairs = width // LANES
    wide = padded(offsets, GROUP)
    wide = padded(wide, 64)
    block = (pairs, LANES)

    ids = lax.dynamic_index_in_dim(send_lists, me, 0, keepdims=False).reshape(-1) - me * batches
    own, outgoing = pl.pallas_call(
        pack_kernel,
        out_shape=(
            jax.ShapeDtypeStruct((batches,) + block, BF16),
            jax.ShapeDtypeStruct((devices * slots,) + block, BF16),
        ),
        in_specs=[SMEM, VMEM],
        out_specs=(VMEM, VMEM),
        scratch_shapes=[pltpu.VMEM((batches * pairs, LANES), F32)],
        compiler_params=params(16),
        name="pack",
    )(ids, multipoles)
    arrived = lax.all_to_all(outgoing, axes, split_axis=0, concat_axis=0, tiled=True)
    up = [(i, i + 1) for i in range(devices - 1)]
    before = lax.ppermute(own, axes, up)
    after = lax.ppermute(own, axes, [(j, i) for i, j in up])

    tall = padded(batches + 1, 8)
    near_tbl, far_slot, far_off, far_items = pl.pallas_call(
        functools.partial(table_kernel, batches * devices),
        out_shape=(
            jax.ShapeDtypeStruct((batches, wide), I32),
            jax.ShapeDtypeStruct((tall, wide), I32),
            jax.ShapeDtypeStruct((tall, wide), I32),
            jax.ShapeDtypeStruct((tall, LANES), I32),
        ),
        in_specs=[SMEM, VMEM, VMEM, VMEM],
        out_specs=(VMEM,) * 4,
        compiler_params=params(16),
        name="tables",
    )(((me - 1) * batches).reshape(1), pair_source, pair_offset, live_pairs.reshape(batches, 1))

    ops = operators.transpose(0, 2, 1)
    near = pl.pallas_call(
        near_kernel,
        out_shape=jax.ShapeDtypeStruct((batches,) + block, F32),
        in_specs=[SMEM] + [VMEM] * 4,
        out_specs=VMEM,
        scratch_shapes=[pltpu.VMEM((3 * batches + 1,) + block, BF16)],
        compiler_params=params(24),
        cost_estimate=pl.CostEstimate(flops=12_000_000_000, bytes_accessed=4_000_000, transcendentals=0),
        name="near",
    )(near_tbl, before, own, after, ops)

    occ = jnp.broadcast_to(occupied.astype(F32)[:, :, None], (batches, width // coeffs, coeffs)).reshape(batches, width)
    return pl.pallas_call(
        far_kernel,
        out_shape=jax.ShapeDtypeStruct((batches, width), F32),
        in_specs=[SMEM] * 3 + [VMEM] * 4,
        out_specs=VMEM,
        scratch_shapes=[
            pltpu.VMEM((devices * slots + 1,) + block, BF16),
            pltpu.VMEM((devices * slots + 1,) + block, BF16),
            pltpu.VMEM(((batches + 1) * pairs, LANES), F32),
        ],
        compiler_params=params(32),
        name="far",
    )(far_slot, far_off, far_items, arrived, ops, near, occ)


def solution(mesh):
    spec = P(("key", "lvl"), None)
    return jax.shard_map(
        local,
        mesh=mesh,
        in_specs=(spec, P(), spec, spec, P(("key", "lvl")), P(), spec),
        out_specs=spec,
        check_vma=False,
    )
```

```python
import functools

import jax
import jax.numpy as jnp
from jax import lax
from jax.experimental import pallas as pl
from jax.experimental.pallas import tpu as pltpu
from jax.sharding import PartitionSpec as P

F32 = jnp.float32
BF16 = jnp.bfloat16
I32 = jnp.int32
VMEM = pl.BlockSpec(memory_space=pltpu.VMEM)
SMEM = pl.BlockSpec(memory_space=pltpu.SMEM)
GROUP = 8
FEW = 8
ITEMS = 8
LANES = 128
NT = (((1,), (1,)), ((), ()))


def params(mib):
    return pltpu.CompilerParams(vmem_limit_bytes=mib << 20)


def padded(n, m):
    return -(-n // m) * m


def pack_kernel(me, send, m_hbm, own, outgoing, m, ids, scr, sems):
    batches, pairs = own.shape[0], own.shape[1]
    slots, devices = ids.shape
    rows = pltpu.make_async_copy(m_hbm, m, sems.at[0])
    lists = pltpu.make_async_copy(send.at[me[0]], ids, sems.at[1])
    rows.start()
    lists.start()
    rows.wait()
    for i in range(pairs):
        for h in range(0, batches, 16):
            x = m[h : h + 16, i * LANES : (i + 1) * LANES].astype(F32)
            scr[pl.ds(h * pairs + i, 16, stride=pairs), :] = x
    for b in range(batches):
        own[b] = scr[b * pairs : (b + 1) * pairs, :].astype(BF16)
    lists.wait()
    first = me[0] * batches

    def send_to(j, _):
        for k in range(slots):
            outgoing[j * slots + k] = own[ids[k, j] - first]
        return 0

    lax.fori_loop(0, devices, send_to, 0, unroll=8)


def ops_kernel(native, twice, scr):
    coeffs, offsets = native.shape[0], native.shape[2]
    half = coeffs // 2
    low = lax.broadcasted_iota(I32, (half, LANES), 1) < coeffs
    for i in range(half):
        x = jnp.concatenate([native[i], native[half + i]], axis=0).astype(F32)
        scr[pl.ds(i, offsets, stride=half), :] = x.T

    def spread(l, _):
        x = scr[pl.ds(pl.multiple_of(l * half, half), half), :]
        y = pltpu.roll(x, coeffs, 1)
        twice[l, 0:half] = jnp.where(low, x, y).astype(BF16)
        twice[l, half:coeffs] = jnp.where(low, y, x).astype(BF16)
        return 0

    lax.fori_loop(0, offsets, spread, 0, unroll=7)


def table_kernel(total_batches, base, src, off, live, near_tbl, far_slot, far_off, far_items):
    rows, lst = src.shape
    wide = near_tbl.shape[1]
    s = src[...]
    o = off[...]
    mine = base[0]
    twin = base[1]
    other = base[2]
    at_r = lax.broadcasted_iota(I32, (rows, rows), 0)
    at_c = lax.broadcasted_iota(I32, (rows, rows), 1)
    count_col = jnp.sum(jnp.where(at_r == at_c, live[...], 0), axis=1, keepdims=True)
    col = lax.broadcasted_iota(I32, (rows, lst), 1)
    alive = col < count_col
    far = s >= total_batches
    in_mine = (s >= mine) & (s < mine + rows)
    in_twin = (s >= twin) & (s < twin + rows)
    place = jnp.where(in_mine, s - mine, jnp.where(in_twin, s - twin + rows, s - other + 2 * rows))
    near_val = jnp.where(alive & jnp.logical_not(far), place + 1, 0)
    far_live = alive & far
    far_val = jnp.where(far_live, s - total_batches + 1, 0)
    one = jnp.where(far_live, 1.0, 0.0)
    before = lax.broadcasted_iota(I32, (lst, lst), 0) < lax.broadcasted_iota(I32, (lst, lst), 1)
    rank = jnp.dot(one.astype(BF16), jnp.where(before, 1.0, 0.0).astype(BF16), preferred_element_type=F32)
    pos = jnp.where(far_live, rank.astype(I32), wide)
    count = jnp.sum(one, axis=1, keepdims=True).astype(I32)
    items = jnp.maximum((count + (FEW - 1)) // FEW, 1)
    far_items[...] = jnp.ones_like(far_items)
    far_items[0:rows, :] = jnp.broadcast_to(items, (rows, LANES))
    near_b = near_val.astype(F32).astype(BF16)
    far_b = jnp.concatenate([far_val & 127, far_val >> 7, o], axis=0).astype(F32).astype(BF16)
    want = lax.broadcasted_iota(I32, (wide, lst), 0)
    far_slot[...] = jnp.zeros_like(far_slot)
    far_off[...] = jnp.zeros_like(far_off)
    for t in range(rows):
        hot = jnp.where(want == o[t : t + 1, :], 1.0, 0.0).astype(BF16)
        got = lax.dot_general(near_b, hot, NT, preferred_element_type=F32)
        near_tbl[t : t + 1, :] = got[t : t + 1, :].astype(I32)
        hot = jnp.where(want == pos[t : t + 1, :], 1.0, 0.0).astype(BF16)
        got = lax.dot_general(far_b, hot, NT, preferred_element_type=F32).astype(I32)
        far_slot[t : t + 1, :] = got[t : t + 1, :] + 128 * got[rows + t : rows + t + 1, :]
        far_off[t : t + 1, :] = got[2 * rows + t : 2 * rows + t + 1, :]


def near_kernel(tbl, own, twin, other, ops, acc, pool):
    batches = own.shape[0]
    last = ops.shape[0] - 1
    zero = jnp.zeros(pool.shape[1:], BF16)
    pool[0] = zero
    for n, part in enumerate((own, twin, other)):
        for b in range(batches):
            pool[1 + n * batches + b] = part[b]
    acc[...] = jnp.zeros_like(acc)
    blank = jnp.zeros(ops.shape[1:], BF16)
    low = lax.broadcasted_iota(I32, blank.shape, 1) < blank.shape[0]

    def group(g, _):
        blocks = []
        for h in range(GROUP):
            op = ops[jnp.minimum(g * GROUP + h, last)]
            blocks.append(jnp.concatenate([jnp.where(low, op, blank), jnp.where(low, blank, op)], axis=0))
        w = jnp.concatenate(blocks, axis=1)
        rows = []
        for t in range(batches):
            rows.append(jnp.concatenate([pool[tbl[t, g * GROUP + h]] for h in range(GROUP)], axis=1))
        x = jnp.concatenate(rows, axis=0)
        acc[...] += lax.dot_general(x, w, NT, preferred_element_type=F32).reshape(acc.shape)
        return 0

    lax.fori_loop(0, tbl.shape[1] // GROUP, group, 0)


def far_kernel(slots, offs, items, arrived, ops, near, occ, out, pool, acc):
    batches, pairs = near.shape[0], near.shape[1]
    half = ops.shape[1]
    pool[0] = jnp.zeros(pool.shape[1:], BF16)

    def fill(n, _):
        x = arrived[n]
        pool[n + 1, 0:pairs] = x
        pool[n + 1, pairs : 2 * pairs] = jnp.concatenate([x[:, half:], x[:, :half]], axis=1)
        return 0

    lax.fori_loop(0, arrived.shape[0], fill, 0, unroll=8)
    acc[0 : batches * pairs, :] = near[...].reshape(batches * pairs, LANES)
    acc[batches * pairs :, :] = jnp.zeros((pairs, LANES), F32)
    low = lax.broadcasted_iota(I32, (pairs, LANES), 1) < half
    low_op = lax.broadcasted_iota(I32, (half, LANES), 1) < half
    total = lax.fori_loop(0, batches, lambda t, n: n + items[t, 0], 0)

    def step(i, place):
        t, g = place
        for u in range(ITEMS):
            xs, ws = [], []
            for h in range(0, FEW, 2):
                e = g * FEW + h
                a, b = slots[t, e], slots[t, e + 1]
                even = jnp.where(low, pool[a, 0:pairs], pool[b, pairs : 2 * pairs])
                odd = jnp.where(low, pool[a, pairs : 2 * pairs], pool[b, 0:pairs])
                xs.append(jnp.concatenate([even, odd], axis=0))
                ws.append(jnp.where(low_op, ops[offs[t, e]], ops[offs[t, e + 1]]))
            r = lax.dot_general(jnp.concatenate(xs, axis=1), jnp.concatenate(ws, axis=1), NT, preferred_element_type=F32)
            at = pl.ds(pl.multiple_of(t * pairs, pairs), pairs)
            acc[at, :] += jnp.concatenate([r[:pairs], r[pairs:]], axis=1)
            end = g + 1 >= items[t, 0]
            t = jnp.where(end, jnp.minimum(t + 1, batches), t)
            g = jnp.where(end, 0, g + 1)
        return t, g

    lax.fori_loop(0, (total + (ITEMS - 1)) // ITEMS, step, (jnp.int32(0), jnp.int32(0)))
    cells = occ.shape[1]
    filled = occ[...].astype(F32).astype(BF16)
    cell = lax.broadcasted_iota(I32, (cells, LANES), 0)
    upper = (lax.broadcasted_iota(I32, (cells, LANES), 1) >= half).astype(I32)
    for i in range(pairs):
        spread = jnp.where(cell == upper + 2 * i, 1.0, 0.0).astype(BF16)
        keep = jnp.dot(filled, spread, preferred_element_type=F32)
        out[:, i * LANES : (i + 1) * LANES] = acc[pl.ds(i, batches, stride=pairs), :] * keep


def local(multipoles, operators, pair_source, pair_offset, live_pairs, send_lists, occupied):
    axes = ("key", "lvl")
    batches, width = multipoles.shape
    offsets, coeffs = operators.shape[0], operators.shape[1]
    devices = lax.axis_size(axes)
    slots = send_lists.shape[2]
    me = lax.axis_index(axes)
    pairs = width // LANES
    wide = padded(offsets, GROUP)
    wide = padded(wide, 64)
    block = (pairs, LANES)

    any_space = pl.BlockSpec(memory_space=pl.ANY)
    own, outgoing = pl.pallas_call(
        pack_kernel,
        out_shape=(
            jax.ShapeDtypeStruct((batches,) + block, BF16),
            jax.ShapeDtypeStruct((devices * slots,) + block, BF16),
        ),
        in_specs=[SMEM, any_space, any_space],
        out_specs=(VMEM, VMEM),
        scratch_shapes=[
            pltpu.VMEM((batches, width), BF16),
            pltpu.SMEM((slots, devices), I32),
            pltpu.VMEM((batches * pairs, LANES), F32),
            pltpu.SemaphoreType.DMA((2,)),
        ],
        compiler_params=params(16),
        name="pack",
    )(me.reshape(1), send_lists.transpose(0, 2, 1), multipoles)
    even = [(i, i ^ 1) for i in range(devices)]
    odd = [p for i in range(1, devices - 1, 2) for p in ((i, i + 1), (i + 1, i))]
    arrived = lax.all_to_all(outgoing, axes, split_axis=0, concat_axis=0, tiled=True)
    twin = lax.ppermute(own, axes, even)
    other = lax.ppermute(own, axes, odd)
    first = jnp.stack([me, me ^ 1, me - 1 + 2 * (me & 1)]) * batches

    tall = padded(batches + 1, 8)
    near_tbl, far_slot, far_off, far_items = pl.pallas_call(
        functools.partial(table_kernel, batches * devices),
        out_shape=(
            jax.ShapeDtypeStruct((batches, wide), I32),
            jax.ShapeDtypeStruct((tall, wide), I32),
            jax.ShapeDtypeStruct((tall, wide), I32),
            jax.ShapeDtypeStruct((tall, LANES), I32),
        ),
        in_specs=[SMEM, VMEM, VMEM, VMEM],
        out_specs=(VMEM,) * 4,
        compiler_params=params(16),
        name="tables",
    )(first, pair_source, pair_offset, live_pairs.reshape(1, batches))

    ops = pl.pallas_call(
        ops_kernel,
        out_shape=jax.ShapeDtypeStruct((offsets, coeffs, LANES), BF16),
        in_specs=[VMEM],
        out_specs=VMEM,
        scratch_shapes=[pltpu.VMEM((offsets * coeffs // 2, LANES), F32)],
        compiler_params=params(24),
        name="ops",
    )(operators.transpose(1, 2, 0))
    near = pl.pallas_call(
        near_kernel,
        out_shape=jax.ShapeDtypeStruct((batches,) + block, F32),
        in_specs=[SMEM] + [VMEM] * 4,
        out_specs=VMEM,
        scratch_shapes=[pltpu.VMEM((3 * batches + 1,) + block, BF16)],
        compiler_params=params(24),
        cost_estimate=pl.CostEstimate(flops=12_000_000_000, bytes_accessed=4_000_000, transcendentals=0),
        name="near",
    )(near_tbl, own, twin, other, ops)

    return pl.pallas_call(
        far_kernel,
        out_shape=jax.ShapeDtypeStruct((batches, width), F32),
        in_specs=[SMEM] * 3 + [VMEM] * 4,
        out_specs=VMEM,
        scratch_shapes=[
            pltpu.VMEM((devices * slots + 1, 2 * pairs, LANES), BF16),
            pltpu.VMEM(((batches + 1) * pairs, LANES), F32),
        ],
        compiler_params=params(32),
        name="far",
    )(far_slot, far_off, far_items, arrived, ops, near, occupied)


def solution(mesh):
    spec = P(("key", "lvl"), None)
    return jax.shard_map(
        local,
        mesh=mesh,
        in_specs=(spec, P(), spec, spec, P(("key", "lvl")), P(), spec),
        out_specs=spec,
        check_vma=False,
    )
```

```python
import functools

import jax
import jax.numpy as jnp
from jax import lax
from jax.experimental import pallas as pl
from jax.experimental.pallas import tpu as pltpu
from jax.sharding import PartitionSpec as P

F32 = jnp.float32
BF16 = jnp.bfloat16
I32 = jnp.int32
VMEM = pl.BlockSpec(memory_space=pltpu.VMEM)
SMEM = pl.BlockSpec(memory_space=pltpu.SMEM)
HBM = pl.BlockSpec(memory_space=pltpu.HBM)
GROUP = 16
FEW = 8
ITEMS = 16
LANES = 128
NT = (((1,), (1,)), ((), ()))


def params(mib):
    return pltpu.CompilerParams(vmem_limit_bytes=mib << 20)


def padded(n, m):
    return -(-n // m) * m


def pack_kernel(me, send, m_hbm, own, outgoing, m, ids, scr, sems):
    batches, pairs = own.shape[0], own.shape[1]
    slots, devices = ids.shape
    rows = pltpu.make_async_copy(m_hbm, m, sems.at[0])
    lists = pltpu.make_async_copy(send.at[me[0]], ids, sems.at[1])
    rows.start()
    lists.start()
    rows.wait()
    for i in range(pairs):
        for h in range(0, batches, 16):
            x = m[h : h + 16, i * LANES : (i + 1) * LANES].astype(F32)
            scr[pl.ds(h * pairs + i, 16, stride=pairs), :] = x
    for b in range(batches):
        own[b] = scr[b * pairs : (b + 1) * pairs, :].astype(BF16)
    lists.wait()
    first = me[0] * batches

    def send_to(j, _):
        for k in range(slots):
            outgoing[j * slots + k] = own[ids[k, j] - first]
        return 0

    lax.fori_loop(0, devices, send_to, 0, unroll=8)


def spread_ops(native, twice, scr):
    coeffs, offsets = native.shape[0], native.shape[2]
    half = coeffs // 2
    tall = twice.shape[0]
    at = lax.broadcasted_iota(I32, (tall, offsets), 0)
    eye = jnp.where(at == lax.broadcasted_iota(I32, (tall, offsets), 1), 1.0, 0.0).astype(BF16)
    for i in range(0, half, 2):
        x = jnp.concatenate([native[i], native[half + i], native[i + 1], native[half + i + 1]], axis=0)
        y = lax.dot_general(eye, x, NT, preferred_element_type=F32)
        scr[pl.ds(i, tall, stride=half), :] = y[:, :LANES]
        scr[pl.ds(i + 1, tall, stride=half), :] = y[:, LANES:]
    low = lax.broadcasted_iota(I32, (half, LANES), 1) < coeffs

    def spread(l, _):
        x = scr[pl.ds(pl.multiple_of(l * half, half), half), :]
        y = pltpu.roll(x, coeffs, 1)
        twice[l, 0:half] = jnp.where(low, x, y).astype(BF16)
        twice[l, half:coeffs] = jnp.where(low, y, x).astype(BF16)
        return 0

    lax.fori_loop(0, tall, spread, 0, unroll=8)


def make_tables(total_batches, base, src, off, live, near_tbl, far_slot, far_off, far_items):
    rows, lst = src.shape
    wide = near_tbl.shape[1]
    s = src[...]
    o = off[...]
    mine = base[0]
    twin = base[1]
    other = base[2]
    at_r = lax.broadcasted_iota(I32, (rows, rows), 0)
    at_c = lax.broadcasted_iota(I32, (rows, rows), 1)
    count_col = jnp.sum(jnp.where(at_r == at_c, live[...], 0), axis=1, keepdims=True)
    col = lax.broadcasted_iota(I32, (rows, lst), 1)
    alive = col < count_col
    far = s >= total_batches
    in_mine = (s >= mine) & (s < mine + rows)
    in_twin = (s >= twin) & (s < twin + rows)
    place = jnp.where(in_mine, s - mine, jnp.where(in_twin, s - twin + rows, s - other + 2 * rows))
    near_val = jnp.where(alive & jnp.logical_not(far), place + 1, 0)
    far_live = alive & far
    far_val = jnp.where(far_live, s - total_batches + 1, 0)
    one = jnp.where(far_live, 1.0, 0.0)
    before = lax.broadcasted_iota(I32, (lst, lst), 0) < lax.broadcasted_iota(I32, (lst, lst), 1)
    rank = jnp.dot(one.astype(BF16), jnp.where(before, 1.0, 0.0).astype(BF16), preferred_element_type=F32)
    pos = jnp.where(far_live, rank.astype(I32), wide)
    count = jnp.sum(one, axis=1, keepdims=True).astype(I32)
    items = jnp.maximum((count + (FEW - 1)) // FEW, 1)
    far_items[...] = jnp.ones_like(far_items)
    far_items[0:rows, :] = jnp.broadcast_to(items, (rows, LANES))
    near_b = near_val.astype(F32).astype(BF16)
    far_b = jnp.concatenate([far_val & 127, far_val >> 7, o], axis=0).astype(F32).astype(BF16)
    want = lax.broadcasted_iota(I32, (wide, lst), 0)
    far_slot[...] = jnp.zeros_like(far_slot)
    far_off[...] = jnp.zeros_like(far_off)
    for t in range(rows):
        hot = jnp.where(want == o[t : t + 1, :], 1.0, 0.0).astype(BF16)
        got = lax.dot_general(near_b, hot, NT, preferred_element_type=F32)
        near_tbl[t : t + 1, :] = got[t : t + 1, :].astype(I32)
        hot = jnp.where(want == pos[t : t + 1, :], 1.0, 0.0).astype(BF16)
        got = lax.dot_general(far_b, hot, NT, preferred_element_type=F32).astype(I32)
        far_slot[t : t + 1, :] = got[t : t + 1, :] + 128 * got[rows + t : rows + t + 1, :]
        far_off[t : t + 1, :] = got[2 * rows + t : 2 * rows + t + 1, :]


def near_kernel(
    total_batches, base, src, off, live, native_hbm, own, twin, other,
    sums, ops, far_slot, far_off, far_items,
    native, scr, tbl_v, tbl, pool, acc, sems,
):
    fetch = pltpu.make_async_copy(native_hbm, native, sems.at[0])
    fetch.start()
    make_tables(total_batches, base, src, off, live, tbl_v, far_slot, far_off, far_items)
    to_smem = pltpu.make_async_copy(tbl_v, tbl, sems.at[1])
    to_smem.start()
    batches = own.shape[0]
    pool[0] = jnp.zeros(pool.shape[1:], BF16)
    for n, part in enumerate((own, twin, other)):
        for b in range(batches):
            pool[1 + n * batches + b] = part[b]
    acc[...] = jnp.zeros_like(acc)
    fetch.wait()
    spread_ops(native, ops, scr)
    to_smem.wait()
    blank = jnp.zeros(ops.shape[1:], BF16)
    low = lax.broadcasted_iota(I32, blank.shape, 1) < blank.shape[0]

    def group(g, _):
        blocks = []
        for h in range(GROUP):
            op = ops[g * GROUP + h]
            blocks.append(jnp.concatenate([jnp.where(low, op, blank), jnp.where(low, blank, op)], axis=0))
        w = jnp.concatenate(blocks, axis=1)
        rows = []
        for t in range(batches):
            rows.append(jnp.concatenate([pool[tbl[t, g * GROUP + h]] for h in range(GROUP)], axis=1))
        x = jnp.concatenate(rows, axis=0)
        acc[...] += lax.dot_general(x, w, NT, preferred_element_type=F32).reshape(acc.shape)
        return 0

    lax.fori_loop(0, tbl.shape[1] // GROUP, group, 0)
    done = pltpu.make_async_copy(acc, sums, sems.at[0])
    done.start()
    done.wait()


def far_kernel(slots, offs, items, arrived_hbm, ops, near_hbm, occ, out, arrived, near, pool, acc, sems):
    batches, pairs = near.shape[0], near.shape[1]
    fetch = pltpu.make_async_copy(arrived_hbm, arrived, sems.at[0])
    fetch_near = pltpu.make_async_copy(near_hbm, near, sems.at[1])
    fetch.start()
    fetch_near.start()
    acc[...] = jnp.zeros_like(acc)
    fetch.wait()
    half = ops.shape[1]
    pool[0] = jnp.zeros(pool.shape[1:], BF16)

    def fill(n, _):
        x = arrived[n]
        pool[n + 1, 0:pairs] = x
        pool[n + 1, pairs : 2 * pairs] = jnp.concatenate([x[:, half:], x[:, :half]], axis=1)
        return 0

    lax.fori_loop(0, arrived.shape[0], fill, 0, unroll=8)
    low = lax.broadcasted_iota(I32, (pairs, LANES), 1) < half
    low_op = lax.broadcasted_iota(I32, (half, LANES), 1) < half
    total = lax.fori_loop(0, batches, lambda t, n: n + items[t, 0], 0)

    def step(i, place):
        t, g = place
        for u in range(ITEMS):
            xs, ws = [], []
            for h in range(0, FEW, 2):
                e = g * FEW + h
                a, b = slots[t, e], slots[t, e + 1]
                even = jnp.where(low, pool[a, 0:pairs], pool[b, pairs : 2 * pairs])
                odd = jnp.where(low, pool[a, pairs : 2 * pairs], pool[b, 0:pairs])
                xs.append(jnp.concatenate([even, odd], axis=0))
                ws.append(jnp.where(low_op, ops[offs[t, e]], ops[offs[t, e + 1]]))
            r = lax.dot_general(jnp.concatenate(xs, axis=1), jnp.concatenate(ws, axis=1), NT, preferred_element_type=F32)
            at = pl.ds(pl.multiple_of(t * pairs, pairs), pairs)
            acc[at, :] += jnp.concatenate([r[:pairs], r[pairs:]], axis=1)
            end = g + 1 >= items[t, 0]
            t = jnp.where(end, jnp.minimum(t + 1, batches), t)
            g = jnp.where(end, 0, g + 1)
        return t, g

    lax.fori_loop(0, (total + (ITEMS - 1)) // ITEMS, step, (jnp.int32(0), jnp.int32(0)))
    fetch_near.wait()

    def join(t, _):
        at = pl.ds(pl.multiple_of(t * pairs, pairs), pairs)
        acc[at, :] += near[t]
        return 0

    lax.fori_loop(0, batches, join, 0, unroll=8)
    cells = occ.shape[1]
    filled = occ[...].astype(F32).astype(BF16)
    cell = lax.broadcasted_iota(I32, (cells, LANES), 0)
    upper = (lax.broadcasted_iota(I32, (cells, LANES), 1) >= half).astype(I32)
    for i in range(pairs):
        spread = jnp.where(cell == upper + 2 * i, 1.0, 0.0).astype(BF16)
        keep = jnp.dot(filled, spread, preferred_element_type=F32)
        out[:, i * LANES : (i + 1) * LANES] = acc[pl.ds(i, batches, stride=pairs), :] * keep


def local(multipoles, operators, pair_source, pair_offset, live_pairs, send_lists, occupied):
    axes = ("key", "lvl")
    batches, width = multipoles.shape
    offsets, coeffs = operators.shape[0], operators.shape[1]
    devices = lax.axis_size(axes)
    slots = send_lists.shape[2]
    me = lax.axis_index(axes)
    pairs = width // LANES
    wide = padded(offsets, GROUP)
    wide = padded(wide, 64)
    block = (pairs, LANES)

    own, outgoing = pl.pallas_call(
        pack_kernel,
        out_shape=(
            jax.ShapeDtypeStruct((batches,) + block, BF16),
            jax.ShapeDtypeStruct((devices * slots,) + block, BF16),
        ),
        in_specs=[SMEM, HBM, HBM],
        out_specs=(VMEM, VMEM),
        scratch_shapes=[
            pltpu.VMEM((batches, width), BF16),
            pltpu.SMEM((slots, devices), I32),
            pltpu.VMEM((batches * pairs, LANES), F32),
            pltpu.SemaphoreType.DMA((2,)),
        ],
        compiler_params=params(16),
        name="pack",
    )(me.reshape(1), send_lists.transpose(0, 2, 1), multipoles)
    even = [(i, i ^ 1) for i in range(devices)]
    odd = [p for i in range(1, devices - 1, 2) for p in ((i, i + 1), (i + 1, i))]
    arrived = lax.all_to_all(outgoing, axes, split_axis=0, concat_axis=0, tiled=True)
    twin = lax.ppermute(own, axes, even)
    other = lax.ppermute(own, axes, odd)
    first = jnp.stack([me, me ^ 1, me - 1 + 2 * (me & 1)]) * batches

    tall = padded(batches + 1, 8)
    sums, ops, far_slot, far_off, far_items = pl.pallas_call(
        functools.partial(near_kernel, batches * devices),
        out_shape=(
            jax.ShapeDtypeStruct((batches,) + block, F32),
            jax.ShapeDtypeStruct((wide, coeffs, LANES), BF16),
            jax.ShapeDtypeStruct((tall, wide), I32),
            jax.ShapeDtypeStruct((tall, wide), I32),
            jax.ShapeDtypeStruct((tall, LANES), I32),
        ),
        in_specs=[SMEM, VMEM, VMEM, VMEM, HBM, VMEM, VMEM, VMEM],
        out_specs=(HBM,) + (VMEM,) * 4,
        scratch_shapes=[
            pltpu.VMEM((coeffs, coeffs, offsets), BF16),
            pltpu.VMEM((wide * coeffs // 2, LANES), F32),
            pltpu.VMEM((batches, wide), I32),
            pltpu.SMEM((batches, wide), I32),
            pltpu.VMEM((3 * batches + 1,) + block, BF16),
            pltpu.VMEM((batches,) + block, F32),
            pltpu.SemaphoreType.DMA((2,)),
        ],
        compiler_params=params(28),
        cost_estimate=pl.CostEstimate(flops=12_000_000_000, bytes_accessed=4_000_000, transcendentals=0),
        name="near",
    )(first, pair_source, pair_offset, live_pairs.reshape(1, batches), operators.transpose(1, 2, 0), own, twin, other)

    return pl.pallas_call(
        far_kernel,
        out_shape=jax.ShapeDtypeStruct((batches, width), F32),
        in_specs=[SMEM] * 3 + [HBM, VMEM, HBM, VMEM],
        out_specs=VMEM,
        scratch_shapes=[
            pltpu.VMEM((devices * slots,) + block, BF16),
            pltpu.VMEM((batches,) + block, F32),
            pltpu.VMEM((devices * slots + 1, 2 * pairs, LANES), BF16),
            pltpu.VMEM(((batches + 1) * pairs, LANES), F32),
            pltpu.SemaphoreType.DMA((2,)),
        ],
        compiler_params=params(32),
        name="far",
    )(far_slot, far_off, far_items, arrived, ops, sums, occupied)


def solution(mesh):
    spec = P(("key", "lvl"), None)
    return jax.shard_map(
        local,
        mesh=mesh,
        in_specs=(spec, P(), spec, spec, P(("key", "lvl")), P(), spec),
        out_specs=spec,
        check_vma=False,
    )
```

```python
import functools

import jax
import jax.numpy as jnp
from jax import lax
from jax.experimental import pallas as pl
from jax.experimental.pallas import tpu as pltpu
from jax.sharding import PartitionSpec as P

F32 = jnp.float32
BF16 = jnp.bfloat16
I32 = jnp.int32
VMEM = pl.BlockSpec(memory_space=pltpu.VMEM)
SMEM = pl.BlockSpec(memory_space=pltpu.SMEM)
HBM = pl.BlockSpec(memory_space=pltpu.HBM)
GROUP = 16
SLOTS = 16
FEW = 8
ITEMS = 16
LANES = 128
NT = (((1,), (1,)), ((), ()))


def params(mib):
    return pltpu.CompilerParams(vmem_limit_bytes=mib << 20)


def padded(n, m):
    return -(-n // m) * m


def pack_kernel(me, send, m_hbm, own, outgoing, m, ids, scr, sems):
    batches, pairs = own.shape[0], own.shape[1]
    slots, devices = ids.shape
    rows = pltpu.make_async_copy(m_hbm, m, sems.at[0])
    lists = pltpu.make_async_copy(send.at[me[0]], ids, sems.at[1])
    rows.start()
    lists.start()
    rows.wait()
    for i in range(pairs):
        for h in range(0, batches, 16):
            x = m[h : h + 16, i * LANES : (i + 1) * LANES].astype(F32)
            scr[pl.ds(h * pairs + i, 16, stride=pairs), :] = x
    for b in range(batches):
        own[b] = scr[b * pairs : (b + 1) * pairs, :].astype(BF16)
    lists.wait()
    first = me[0] * batches

    def send_to(j, _):
        for k in range(slots):
            outgoing[j * slots + k] = own[ids[k, j] - first]
        return 0

    lax.fori_loop(0, devices, send_to, 0, unroll=8)


def spread_ops(native, twice, scr):
    coeffs, offsets = native.shape[0], native.shape[2]
    half = coeffs // 2
    tall = twice.shape[0]
    at = lax.broadcasted_iota(I32, (tall, offsets), 0)
    eye = jnp.where(at == lax.broadcasted_iota(I32, (tall, offsets), 1), 1.0, 0.0).astype(BF16)
    for i in range(0, half, 8):
        found = []
        for k in range(i, i + 8, 2):
            x = jnp.concatenate([native[k], native[half + k], native[k + 1], native[half + k + 1]], axis=0)
            y = lax.dot_general(eye, x, NT, preferred_element_type=F32)
            found += [y[:, :LANES], y[:, LANES:]]
        scr[:, i : i + 8, :] = jnp.swapaxes(jnp.stack(found, axis=0), 0, 1)
    low = lax.broadcasted_iota(I32, (half, LANES), 1) < coeffs

    def spread(l, _):
        x = scr[l]
        y = pltpu.roll(x, coeffs, 1)
        twice[l, 0:half] = jnp.where(low, x, y).astype(BF16)
        twice[l, half:coeffs] = jnp.where(low, y, x).astype(BF16)
        return 0

    lax.fori_loop(0, tall, spread, 0, unroll=8)


def one_hot(want, row):
    return jnp.where(want == row, 1.0, 0.0).astype(BF16)


def make_tables(total_batches, base, src, off, live, near_slots, late_slot, late_off, late_items):
    rows, lst = src.shape
    slots, wide = SLOTS, near_slots.shape[0]
    s = src[...]
    o = off[...]
    mine = base[0]
    twin = base[1]
    other = base[2]
    at_r = lax.broadcasted_iota(I32, (rows, rows), 0)
    at_c = lax.broadcasted_iota(I32, (rows, rows), 1)
    count_col = jnp.sum(jnp.where(at_r == at_c, live[...], 0), axis=1, keepdims=True)
    alive = lax.broadcasted_iota(I32, (rows, lst), 1) < count_col
    far = s >= total_batches
    in_mine = (s >= mine) & (s < mine + rows)
    in_twin = (s >= twin) & (s < twin + rows)
    place = jnp.where(in_mine, s - mine, jnp.where(in_twin, s - twin + rows, s - other + 2 * rows))
    place = jnp.where(far, s - total_batches + 3 * rows, place)
    value = jnp.where(alive, place + 1, 0)
    both = jnp.concatenate([value & 127, value >> 7], axis=0).astype(F32).astype(BF16)
    want = lax.broadcasted_iota(I32, (wide, lst), 0)
    lows, highs = [], []
    for t in range(rows):
        got = lax.dot_general(both, one_hot(want, o[t : t + 1, :]), NT, preferred_element_type=F32)
        lows.append(got[t : t + 1, :])
        highs.append(got[rows + t : rows + t + 1, :])
    low = jnp.concatenate(lows, axis=0)
    high = jnp.concatenate(highs, axis=0)
    value = (low + 128.0 * high).astype(I32)
    near = (value > 0) & (value <= 3 * rows)
    sooner = jnp.where(at_c < at_r, 1.0, 0.0).astype(BF16)
    rank = jnp.dot(sooner, jnp.where(near, 1.0, 0.0).astype(BF16), preferred_element_type=F32).astype(I32)
    target = lax.broadcasted_iota(I32, (rows, wide), 0)
    sources, targets = [], []
    for r in range(slots):
        sel = near & (rank == r)
        sources.append(jnp.sum(jnp.where(sel, value, 0), axis=0, keepdims=True))
        targets.append(jnp.sum(jnp.where(sel, target - rows, 0), axis=0, keepdims=True) + rows)
    table = jnp.concatenate(sources + targets, axis=0).astype(F32)
    near_slots[:, 0 : 2 * slots] = table.T.astype(I32)
    late = (value > 3 * rows) | (near & (rank >= slots))
    one = jnp.where(late, 1.0, 0.0)
    before = lax.broadcasted_iota(I32, (wide, wide), 0) < lax.broadcasted_iota(I32, (wide, wide), 1)
    order = jnp.dot(one.astype(BF16), jnp.where(before, 1.0, 0.0).astype(BF16), preferred_element_type=F32)
    pos = jnp.where(late, order.astype(I32), wide)
    count = jnp.sum(one, axis=1, keepdims=True).astype(I32)
    items = jnp.maximum((count + (FEW - 1)) // FEW, 1)
    late_items[...] = jnp.ones_like(late_items)
    late_items[0:rows, :] = jnp.broadcast_to(items, (rows, LANES))
    late_slot[...] = jnp.zeros_like(late_slot)
    late_off[...] = jnp.zeros_like(late_off)
    want = lax.broadcasted_iota(I32, (wide, wide), 0)
    offset = lax.broadcasted_iota(I32, (16, wide), 1).astype(F32)
    parts = jnp.concatenate([low, high, offset], axis=0).astype(BF16)
    for t in range(rows):
        got = lax.dot_general(parts, one_hot(want, pos[t : t + 1, :]), NT, preferred_element_type=F32).astype(I32)
        late_slot[t : t + 1, :] = got[t : t + 1, :] + 128 * got[rows + t : rows + t + 1, :]
        late_off[t : t + 1, :] = got[2 * rows : 2 * rows + 1, :]


def near_kernel(
    total_batches, base, src, off, live, native_hbm, own, twin, other,
    sums, ops_hbm, late_slot, late_off, late_items,
    native, scr, ops, slots_v, slot_t, pool, acc_a, acc_b, acc_c, acc_d, sems,
):
    fetch = pltpu.make_async_copy(native_hbm, native, sems.at[0])
    fetch.start()
    make_tables(total_batches, base, src, off, live, slots_v, late_slot, late_off, late_items)
    to_smem = pltpu.make_async_copy(slots_v, slot_t, sems.at[1])
    to_smem.start()
    batches, pairs = own.shape[0], own.shape[1]
    pool[0] = jnp.zeros(pool.shape[1:], BF16)
    for n, part in enumerate((own, twin, other)):
        for b in range(batches):
            pool[1 + n * batches + b] = part[b]
    accs = (acc_a, acc_b, acc_c, acc_d)
    for acc in accs:
        acc[...] = jnp.zeros_like(acc)
    fetch.wait()
    spread_ops(native, ops, scr)
    keep = pltpu.make_async_copy(ops, ops_hbm, sems.at[2])
    keep.start()
    to_smem.wait()
    slots = SLOTS
    blank = jnp.zeros(ops.shape[1:], BF16)
    none = jnp.zeros((2 * blank.shape[0], LANES), BF16)
    low = lax.broadcasted_iota(I32, blank.shape, 1) < blank.shape[0]

    def twice(l):
        op = ops[l]
        return jnp.concatenate([jnp.where(low, op, blank), jnp.where(low, blank, op)], axis=0)

    def group(g, _):
        for h in range(0, GROUP, 2):
            l = g * GROUP + h
            top = jnp.concatenate([twice(l), none], axis=1)
            end = jnp.concatenate([none, twice(l + 1)], axis=1)
            w = jnp.concatenate([top, end], axis=0)
            rows = [jnp.concatenate([pool[slot_t[l, r]], pool[slot_t[l + 1, r]]], axis=1) for r in range(slots)]
            y = lax.dot_general(jnp.concatenate(rows, axis=0), w, NT, preferred_element_type=F32)
            for side in range(2):
                acc = accs[(h % 4) // 2 * 2 + side]
                for r in range(0, slots, 4):
                    ats = [slot_t[l + side, slots + r + k] for k in range(4)]
                    olds = [acc[at] for at in ats]
                    for k in range(4):
                        new = y[(r + k) * pairs : (r + k + 1) * pairs, side * LANES : (side + 1) * LANES]
                        acc[ats[k]] = olds[k] + new
        return 0

    lax.fori_loop(0, slot_t.shape[0] // GROUP, group, 0)

    def join(t, _):
        acc_a[t] = (acc_a[t] + acc_b[t]) + (acc_c[t] + acc_d[t])
        return 0

    lax.fori_loop(0, batches, join, 0, unroll=8)
    done = pltpu.make_async_copy(acc_a.at[0:batches], sums, sems.at[0])
    done.start()
    keep.wait()
    done.wait()


def far_kernel(slots, offs, items, own, twin, other, arrived_hbm, ops_hbm, near_hbm, occ, out, arrived, ops, near, pool, acc, sems):
    batches, pairs = near.shape[0], near.shape[1]
    fetch = pltpu.make_async_copy(arrived_hbm, arrived, sems.at[0])
    fetch_near = pltpu.make_async_copy(near_hbm, near, sems.at[1])
    fetch_ops = pltpu.make_async_copy(ops_hbm, ops, sems.at[2])
    fetch.start()
    fetch_ops.start()
    fetch_near.start()
    acc[...] = jnp.zeros_like(acc)
    half = ops.shape[1]
    pool[0] = jnp.zeros(pool.shape[1:], BF16)

    def fill(part, start):
        def put(n, _):
            x = part[n]
            pool[start + n, 0:pairs] = x
            pool[start + n, pairs : 2 * pairs] = jnp.concatenate([x[:, half:], x[:, :half]], axis=1)
            return 0

        lax.fori_loop(0, part.shape[0], put, 0, unroll=8)

    for n, part in enumerate((own, twin, other)):
        fill(part, 1 + n * batches)
    fetch.wait()
    fill(arrived, 1 + 3 * batches)
    fetch_ops.wait()
    low = lax.broadcasted_iota(I32, (pairs, LANES), 1) < half
    low_op = lax.broadcasted_iota(I32, (half, LANES), 1) < half
    total = lax.fori_loop(0, batches, lambda t, n: n + items[t, 0], 0)

    def step(i, place):
        t, g = place
        for u in range(ITEMS):
            xs, ws = [], []
            for h in range(0, FEW, 2):
                e = g * FEW + h
                a, b = slots[t, e], slots[t, e + 1]
                even = jnp.where(low, pool[a, 0:pairs], pool[b, pairs : 2 * pairs])
                odd = jnp.where(low, pool[a, pairs : 2 * pairs], pool[b, 0:pairs])
                xs.append(jnp.concatenate([even, odd], axis=0))
                ws.append(jnp.where(low_op, ops[offs[t, e]], ops[offs[t, e + 1]]))
            r = lax.dot_general(jnp.concatenate(xs, axis=1), jnp.concatenate(ws, axis=1), NT, preferred_element_type=F32)
            at = pl.ds(pl.multiple_of(t * pairs, pairs), pairs)
            acc[at, :] += jnp.concatenate([r[:pairs], r[pairs:]], axis=1)
            end = g + 1 >= items[t, 0]
            t = jnp.where(end, jnp.minimum(t + 1, batches), t)
            g = jnp.where(end, 0, g + 1)
        return t, g

    lax.fori_loop(0, (total + (ITEMS - 1)) // ITEMS, step, (jnp.int32(0), jnp.int32(0)))
    fetch_near.wait()

    def join(t, _):
        at = pl.ds(pl.multiple_of(t * pairs, pairs), pairs)
        acc[at, :] += near[t]
        return 0

    lax.fori_loop(0, batches, join, 0, unroll=8)
    cells = occ.shape[1]
    filled = occ[...].astype(F32).astype(BF16)
    cell = lax.broadcasted_iota(I32, (cells, LANES), 0)
    upper = (lax.broadcasted_iota(I32, (cells, LANES), 1) >= half).astype(I32)
    for i in range(pairs):
        spread = jnp.where(cell == upper + 2 * i, 1.0, 0.0).astype(BF16)
        keep = jnp.dot(filled, spread, preferred_element_type=F32)
        out[:, i * LANES : (i + 1) * LANES] = acc[pl.ds(i, batches, stride=pairs), :] * keep


def local(multipoles, operators, pair_source, pair_offset, live_pairs, send_lists, occupied):
    axes = ("key", "lvl")
    batches, width = multipoles.shape
    offsets, coeffs = operators.shape[0], operators.shape[1]
    devices = lax.axis_size(axes)
    slots = send_lists.shape[2]
    me = lax.axis_index(axes)
    pairs = width // LANES
    wide = padded(offsets, GROUP)
    wide = padded(wide, 64)
    block = (pairs, LANES)

    own, outgoing = pl.pallas_call(
        pack_kernel,
        out_shape=(
            jax.ShapeDtypeStruct((batches,) + block, BF16),
            jax.ShapeDtypeStruct((devices * slots,) + block, BF16),
        ),
        in_specs=[SMEM, HBM, HBM],
        out_specs=(VMEM, VMEM),
        scratch_shapes=[
            pltpu.VMEM((batches, width), BF16),
            pltpu.SMEM((slots, devices), I32),
            pltpu.VMEM((batches * pairs, LANES), F32),
            pltpu.SemaphoreType.DMA((2,)),
        ],
        compiler_params=params(56),
        name="pack",
    )(me.reshape(1), send_lists.transpose(0, 2, 1), multipoles)
    even = [(i, i ^ 1) for i in range(devices)]
    odd = [p for i in range(1, devices - 1, 2) for p in ((i, i + 1), (i + 1, i))]
    arrived = lax.all_to_all(outgoing, axes, split_axis=0, concat_axis=0, tiled=True)
    twin = lax.ppermute(own, axes, even)
    other = lax.ppermute(own, axes, odd)
    first = jnp.stack([me, me ^ 1, me - 1 + 2 * (me & 1)]) * batches

    tall = padded(batches + 1, 8)
    sums, ops, late_slot, late_off, late_items = pl.pallas_call(
        functools.partial(near_kernel, batches * devices),
        out_shape=(
            jax.ShapeDtypeStruct((batches,) + block, F32),
            jax.ShapeDtypeStruct((wide, coeffs, LANES), BF16),
            jax.ShapeDtypeStruct((tall, wide), I32),
            jax.ShapeDtypeStruct((tall, wide), I32),
            jax.ShapeDtypeStruct((tall, LANES), I32),
        ),
        in_specs=[SMEM, VMEM, VMEM, VMEM, HBM, VMEM, VMEM, VMEM],
        out_specs=(HBM, HBM) + (VMEM,) * 3,
        scratch_shapes=[
            pltpu.VMEM((coeffs, coeffs, offsets), BF16),
            pltpu.VMEM((wide, coeffs // 2, LANES), F32),
            pltpu.VMEM((wide, coeffs, LANES), BF16),
            pltpu.VMEM((wide, LANES), I32),
            pltpu.SMEM((wide, LANES), I32),
            pltpu.VMEM((3 * batches + 1,) + block, BF16),
        ]
        + [pltpu.VMEM((batches + 1,) + block, F32)] * 4
        + [
            pltpu.SemaphoreType.DMA((3,)),
        ],
        compiler_params=params(56),
        cost_estimate=pl.CostEstimate(flops=12_000_000_000, bytes_accessed=4_000_000, transcendentals=0),
        name="near",
    )(first, pair_source, pair_offset, live_pairs.reshape(1, batches), operators.transpose(1, 2, 0), own, twin, other)

    return pl.pallas_call(
        far_kernel,
        out_shape=jax.ShapeDtypeStruct((batches, width), F32),
        in_specs=[SMEM] * 3 + [VMEM] * 3 + [HBM] * 3 + [VMEM],
        out_specs=VMEM,
        scratch_shapes=[
            pltpu.VMEM((devices * slots,) + block, BF16),
            pltpu.VMEM((wide, coeffs, LANES), BF16),
            pltpu.VMEM((batches,) + block, F32),
            pltpu.VMEM((3 * batches + devices * slots + 1, 2 * pairs, LANES), BF16),
            pltpu.VMEM(((batches + 1) * pairs, LANES), F32),
            pltpu.SemaphoreType.DMA((3,)),
        ],
        compiler_params=params(56),
        name="far",
    )(late_slot, late_off, late_items, own, twin, other, arrived, ops, sums, occupied)


def solution(mesh):
    spec = P(("key", "lvl"), None)
    return jax.shard_map(
        local,
        mesh=mesh,
        in_specs=(spec, P(), spec, spec, P(("key", "lvl")), P(), spec),
        out_specs=spec,
        check_vma=False,
    )
```

```python
import functools

import jax
import jax.numpy as jnp
from jax import lax
from jax.experimental import pallas as pl
from jax.experimental.pallas import tpu as pltpu
from jax.sharding import PartitionSpec as P

F32 = jnp.float32
BF16 = jnp.bfloat16
I32 = jnp.int32
VMEM = pl.BlockSpec(memory_space=pltpu.VMEM)
SMEM = pl.BlockSpec(memory_space=pltpu.SMEM)
HBM = pl.BlockSpec(memory_space=pltpu.HBM)
GROUP = 32
SLOTS = 16
FEW = 8
ITEMS = 24
LANES = 128
NT = (((1,), (1,)), ((), ()))


def params(mib):
    return pltpu.CompilerParams(vmem_limit_bytes=mib << 20)


def padded(n, m):
    return -(-n // m) * m


def pack_kernel(me, send, m_hbm, own_hbm, outgoing_hbm, m, ids, scr, own, outgoing, sems):
    batches, pairs = own.shape[0], own.shape[1]
    slots, devices = ids.shape
    rows = pltpu.make_async_copy(m_hbm, m, sems.at[0])
    lists = pltpu.make_async_copy(send.at[me[0]], ids, sems.at[1])
    rows.start()
    lists.start()
    rows.wait()
    for i in range(pairs):
        for h in range(0, batches, 16):
            x = m[h : h + 16, i * LANES : (i + 1) * LANES].astype(F32)
            scr[pl.ds(h * pairs + i, 16, stride=pairs), :] = x
    for b in range(batches):
        own[b] = scr[b * pairs : (b + 1) * pairs, :].astype(BF16)
    keep = pltpu.make_async_copy(own, own_hbm, sems.at[2])
    keep.start()
    lists.wait()
    first = me[0] * batches
    part = devices // 4
    done = []
    for c in range(4):

        def send_to(j, _):
            for k in range(slots):
                outgoing[j * slots + k] = own[ids[k, j] - first]
            return 0

        lax.fori_loop(c * part, (c + 1) * part, send_to, 0, unroll=8)
        here = pl.ds(c * part * slots, part * slots)
        done.append(pltpu.make_async_copy(outgoing.at[here], outgoing_hbm.at[here], sems.at[3 + c]))
        done[-1].start()
    keep.wait()
    for copy in done:
        copy.wait()


def turn_ops(native, ops):
    coeffs, offsets = native.shape[0], native.shape[2]
    half = coeffs // 2
    tall = ops.shape[0]
    at = lax.broadcasted_iota(I32, (tall, offsets), 0)
    eye = jnp.where(at == lax.broadcasted_iota(I32, (tall, offsets), 1), 1.0, 0.0).astype(BF16)
    for i in range(0, half, 16):
        blocks = []
        for c in range(i, i + 16, 8):
            found = []
            for k in range(c, c + 8, 2):
                x = jnp.concatenate([native[k], native[half + k], native[k + 1], native[half + k + 1]], axis=0)
                y = lax.dot_general(eye, x, NT, preferred_element_type=F32)
                found += [y[:, :LANES], y[:, LANES:]]
            blocks.append(jnp.swapaxes(jnp.stack(found, axis=0), 0, 1))
        ops[:, i : i + 16, :] = jnp.concatenate(blocks, axis=1).astype(BF16)


def swapped(x):
    half = x.shape[1] // 2
    return jnp.concatenate([x[:, half:], x[:, :half]], axis=1)


def one_hot(want, row):
    return jnp.where(want == row, 1.0, 0.0).astype(BF16)


def make_tables(total_batches, me, src, off, live, near_slots, late):
    rows, lst = src.shape
    slots, wide = SLOTS, near_slots.shape[0]
    s = src[...]
    o = off[...]
    mine = me[0] * rows
    twin = (me[0] ^ 1) * rows
    other = (me[0] - 1 + 2 * (me[0] & 1)) * rows
    at_r = lax.broadcasted_iota(I32, (rows, rows), 0)
    at_c = lax.broadcasted_iota(I32, (rows, rows), 1)
    count_col = jnp.sum(jnp.where(at_r == at_c, live[...], 0), axis=1, keepdims=True)
    alive = lax.broadcasted_iota(I32, (rows, lst), 1) < count_col
    far = s >= total_batches
    in_mine = (s >= mine) & (s < mine + rows)
    in_twin = (s >= twin) & (s < twin + rows)
    place = jnp.where(in_mine, s - mine, jnp.where(in_twin, s - twin + rows, s - other + 2 * rows))
    place = jnp.where(far, s - total_batches + 3 * rows, place)
    value = jnp.where(alive, place + 1, 0)
    both = jnp.concatenate([value & 127, value >> 7], axis=0).astype(F32).astype(BF16)
    want = lax.broadcasted_iota(I32, (wide, lst), 0)
    lows, highs = [], []
    for t in range(rows):
        got = lax.dot_general(both, one_hot(want, o[t : t + 1, :]), NT, preferred_element_type=F32)
        lows.append(got[t : t + 1, :])
        highs.append(got[rows + t : rows + t + 1, :])
    low = jnp.concatenate(lows, axis=0)
    high = jnp.concatenate(highs, axis=0)
    value = (low + 128.0 * high).astype(I32)
    near = (value > 0) & (value <= 3 * rows)
    sooner = jnp.where(at_c < at_r, 1.0, 0.0).astype(BF16)
    rank = jnp.dot(sooner, jnp.where(near, 1.0, 0.0).astype(BF16), preferred_element_type=F32).astype(I32)
    target = lax.broadcasted_iota(I32, (rows, wide), 0)
    sources, targets = [], []
    for r in range(slots):
        sel = near & (rank == r)
        sources.append(jnp.sum(jnp.where(sel, value, 0), axis=0, keepdims=True))
        targets.append(jnp.sum(jnp.where(sel, target - rows, 0), axis=0, keepdims=True) + rows)
    table = jnp.concatenate(sources + targets, axis=0).astype(F32)
    near_slots[:, 0 : 2 * slots] = table.T.astype(I32)
    behind = (value > 3 * rows) | (near & (rank >= slots))
    one = jnp.where(behind, 1.0, 0.0)
    before = lax.broadcasted_iota(I32, (wide, wide), 0) < lax.broadcasted_iota(I32, (wide, wide), 1)
    order = jnp.dot(one.astype(BF16), jnp.where(before, 1.0, 0.0).astype(BF16), preferred_element_type=F32)
    pos = jnp.where(behind, order.astype(I32), wide)
    count = jnp.sum(one, axis=1, keepdims=True).astype(I32)
    items = jnp.maximum((count + (FEW - 1)) // FEW, 1)
    late[:, 0:wide] = jnp.zeros((late.shape[0], wide), I32)
    late[:, wide:] = jnp.ones((late.shape[0], late.shape[1] - wide), I32)
    late[0:rows, wide:] = jnp.broadcast_to(items, (rows, late.shape[1] - wide))
    want = lax.broadcasted_iota(I32, (wide, wide), 0)
    offset = lax.broadcasted_iota(I32, (16, wide), 1).astype(F32)
    parts = jnp.concatenate([low, high, offset], axis=0).astype(BF16)
    for t in range(rows):
        got = lax.dot_general(parts, one_hot(want, pos[t : t + 1, :]), NT, preferred_element_type=F32).astype(I32)
        source = got[t : t + 1, :] + 128 * got[rows + t : rows + t + 1, :]
        late[t : t + 1, 0:wide] = source * 256 + got[2 * rows : 2 * rows + 1, :]


def near_kernel(
    total_batches, me, src_hbm, off_hbm, live_hbm, native_hbm, own, twin, other,
    sums, ops_hbm, late_hbm,
    src, off, live, native, ops, late, slots_v, slot_t, pool, acc_a, acc_b, acc_c, acc_d, sems,
):
    batches, pairs = own.shape[0], own.shape[1]
    lists = []
    for n, (x, y) in enumerate(((src_hbm, src), (off_hbm, off), (live_hbm, live))):
        lists.append(pltpu.make_async_copy(x, y, sems.at[n]))
    fetch = pltpu.make_async_copy(native_hbm, native, sems.at[3])
    parts = []
    for n, part in enumerate((own, twin, other)):
        parts.append(pltpu.make_async_copy(part, pool.at[pl.ds(1 + n * batches, batches)], sems.at[4 + n]))
    for copy in lists + [fetch] + parts:
        copy.start()
    pool[0] = jnp.zeros(pool.shape[1:], BF16)
    accs = (acc_a, acc_b, acc_c, acc_d)
    for acc in accs:
        acc[...] = jnp.zeros_like(acc)
    for copy in lists:
        copy.wait()
    make_tables(total_batches, me, src, off, live, slots_v, late)
    to_smem = pltpu.make_async_copy(slots_v, slot_t, sems.at[7])
    to_smem.start()
    keep_late = pltpu.make_async_copy(late, late_hbm, sems.at[0])
    keep_late.start()
    fetch.wait()
    turn_ops(native, ops)
    keep = pltpu.make_async_copy(ops, ops_hbm, sems.at[1])
    keep.start()
    for copy in parts:
        copy.wait()
    to_smem.wait()
    slots = SLOTS
    blank = jnp.zeros(ops.shape[1:], BF16)
    none = jnp.zeros((LANES, LANES), BF16)
    low = lax.broadcasted_iota(I32, blank.shape, 1) < LANES // 2

    def twice(l):
        x = ops[l]
        y = swapped(x)
        first = [jnp.where(low, x, blank), jnp.where(low, y, blank)]
        return jnp.concatenate(first + [jnp.where(low, blank, y), jnp.where(low, blank, x)], axis=0)

    def group(g, _):
        for h in range(0, GROUP, 2):
            l = g * GROUP + h
            top = jnp.concatenate([twice(l), none], axis=1)
            end = jnp.concatenate([none, twice(l + 1)], axis=1)
            w = jnp.concatenate([top, end], axis=0)
            rows = [jnp.concatenate([pool[slot_t[l, r]], pool[slot_t[l + 1, r]]], axis=1) for r in range(slots)]
            y = lax.dot_general(jnp.concatenate(rows, axis=0), w, NT, preferred_element_type=F32)
            for side in range(2):
                acc = accs[(h % 4) // 2 * 2 + side]
                for r in range(0, slots, 4):
                    ats = [slot_t[l + side, slots + r + k] for k in range(4)]
                    olds = [acc[at] for at in ats]
                    for k in range(4):
                        new = y[(r + k) * pairs : (r + k + 1) * pairs, side * LANES : (side + 1) * LANES]
                        acc[ats[k]] = olds[k] + new
        return 0

    lax.fori_loop(0, slot_t.shape[0] // GROUP, group, 0)

    part = batches // 4
    done = []
    for c in range(4):
        for t in range(c * part, (c + 1) * part):
            acc_a[t] = (acc_a[t] + acc_b[t]) + (acc_c[t] + acc_d[t])
        here = pl.ds(c * part, part)
        done.append(pltpu.make_async_copy(acc_a.at[here], sums.at[here], sems.at[2 + c]))
        done[-1].start()
    keep_late.wait()
    keep.wait()
    for copy in done:
        copy.wait()


def far_kernel(
    table_hbm, own, twin, other, ops_hbm, near_hbm, arrived_hbm, occ_hbm, out_hbm,
    table, blocks, ops, near, occ, pool, acc, out, sems,
):
    batches, pairs = near.shape[0], near.shape[1]
    many = arrived_hbm.shape[0]
    last = table.shape[1] - 1
    fetch_table = pltpu.make_async_copy(table_hbm, table, sems.at[0])
    fetch_ops = pltpu.make_async_copy(ops_hbm, ops, sems.at[1])
    fetch_near = pltpu.make_async_copy(near_hbm, near, sems.at[2])
    fetch_occ = pltpu.make_async_copy(occ_hbm, occ, sems.at[3])
    parts = []
    for n, part in enumerate((own, twin, other, arrived_hbm)):
        here = pl.ds(n * batches, part.shape[0])
        parts.append(pltpu.make_async_copy(part, blocks.at[here], sems.at[4 + n]))
    for copy in [fetch_table] + parts + [fetch_ops, fetch_near, fetch_occ]:
        copy.start()
    acc[...] = jnp.zeros_like(acc)
    pool[0] = jnp.zeros(pool.shape[1:], BF16)
    for copy in parts:
        copy.wait()

    def spread(source, target, start):
        def put(n, _):
            x = source[n]
            target[start + n, 0:pairs] = x
            target[start + n, pairs : 2 * pairs] = swapped(x)
            return 0

        lax.fori_loop(0, source.shape[0], put, 0, unroll=16)

    spread(blocks, pool, 1)
    fetch_table.wait()
    fetch_ops.wait()
    half = LANES // 2
    low = lax.broadcasted_iota(I32, (pairs, LANES), 1) < half
    total = lax.fori_loop(0, batches, lambda t, n: n + table[t, last], 0)

    def step(i, place):
        t, g = place
        for u in range(ITEMS):
            xs, ws = [], []
            for h in range(0, FEW, 2):
                e = g * FEW + h
                va, vb = table[t, e], table[t, e + 1]
                a, b = va >> 8, vb >> 8
                even = jnp.where(low, pool[a, 0:pairs], pool[b, pairs : 2 * pairs])
                odd = jnp.where(low, pool[a, pairs : 2 * pairs], pool[b, 0:pairs])
                xs.append(jnp.concatenate([even, odd], axis=0))
                wa, wb = ops[va & 255], ops[vb & 255]
                ws.append(jnp.concatenate([jnp.where(low, wa, swapped(wb)), jnp.where(low, swapped(wa), wb)], axis=0))
            r = lax.dot_general(jnp.concatenate(xs, axis=1), jnp.concatenate(ws, axis=1), NT, preferred_element_type=F32)
            at = pl.ds(pl.multiple_of(t * pairs, pairs), pairs)
            acc[at, :] += jnp.concatenate([r[:pairs], r[pairs:]], axis=1)
            end = g + 1 >= table[t, last]
            t = jnp.where(end, jnp.minimum(t + 1, batches), t)
            g = jnp.where(end, 0, g + 1)
        return t, g

    lax.fori_loop(0, (total + (ITEMS - 1)) // ITEMS, step, (jnp.int32(0), jnp.int32(0)))
    fetch_near.wait()
    fetch_occ.wait()

    def join(t, _):
        at = pl.ds(pl.multiple_of(t * pairs, pairs), pairs)
        acc[at, :] += near[t]
        return 0

    lax.fori_loop(0, batches, join, 0, unroll=8)
    cells = occ.shape[1]
    filled = occ[...].astype(F32).astype(BF16)
    cell = lax.broadcasted_iota(I32, (cells, LANES), 0)
    odd_cell = (lax.broadcasted_iota(I32, (cells, LANES), 1) >= half).astype(I32)
    done = []
    for i in range(pairs):
        spread = jnp.where(cell == odd_cell + 2 * i, 1.0, 0.0).astype(BF16)
        keep = jnp.dot(filled, spread, preferred_element_type=F32)
        out[:, i * LANES : (i + 1) * LANES] = acc[pl.ds(i, batches, stride=pairs), :] * keep
        if i % 8 == 7:
            here = pl.ds((i - 7) * LANES, 8 * LANES)
            done.append(pltpu.make_async_copy(out.at[:, here], out_hbm.at[:, here], sems.at[i // 8]))
            done[-1].start()
    for copy in done:
        copy.wait()


def local(multipoles, operators, pair_source, pair_offset, live_pairs, send_lists, occupied):
    axes = ("key", "lvl")
    batches, width = multipoles.shape
    offsets, coeffs = operators.shape[0], operators.shape[1]
    devices = lax.axis_size(axes)
    slots = send_lists.shape[2]
    me = lax.axis_index(axes)
    pairs = width // LANES
    wide = padded(offsets, GROUP)
    wide = padded(wide, 64)
    block = (pairs, LANES)

    own, outgoing = pl.pallas_call(
        pack_kernel,
        out_shape=(
            jax.ShapeDtypeStruct((batches,) + block, BF16),
            jax.ShapeDtypeStruct((devices * slots,) + block, BF16),
        ),
        in_specs=[SMEM, HBM, HBM],
        out_specs=(HBM, HBM),
        scratch_shapes=[
            pltpu.VMEM((batches, width), BF16),
            pltpu.SMEM((slots, devices), I32),
            pltpu.VMEM((batches * pairs, LANES), F32),
            pltpu.VMEM((batches,) + block, BF16),
            pltpu.VMEM((devices * slots,) + block, BF16),
            pltpu.SemaphoreType.DMA((7,)),
        ],
        compiler_params=params(56),
        name="pack",
    )(me.reshape(1), send_lists.transpose(0, 2, 1), multipoles)
    even = [(i, i ^ 1) for i in range(devices)]
    odd = [p for i in range(1, devices - 1, 2) for p in ((i, i + 1), (i + 1, i))]
    arrived = lax.all_to_all(outgoing, axes, split_axis=0, concat_axis=0, tiled=True)
    twin = lax.ppermute(own, axes, even)
    other = lax.ppermute(own, axes, odd)
    tall = padded(batches + 1, 8)
    ops_shape = (wide, coeffs // 2, LANES)
    late_shape = (tall, padded(wide + 1, LANES))
    sums, ops, late = pl.pallas_call(
        functools.partial(near_kernel, batches * devices),
        out_shape=(
            jax.ShapeDtypeStruct((batches,) + block, F32),
            jax.ShapeDtypeStruct(ops_shape, BF16),
            jax.ShapeDtypeStruct(late_shape, I32),
        ),
        in_specs=[SMEM] + [HBM] * 7,
        out_specs=(HBM,) * 3,
        scratch_shapes=[
            pltpu.VMEM((batches, offsets), I32),
            pltpu.VMEM((batches, offsets), I32),
            pltpu.VMEM((1, batches), I32),
            pltpu.VMEM((coeffs, coeffs, offsets), BF16),
            pltpu.VMEM(ops_shape, BF16),
            pltpu.VMEM(late_shape, I32),
            pltpu.VMEM((wide, LANES), I32),
            pltpu.SMEM((wide, LANES), I32),
            pltpu.VMEM((3 * batches + 1,) + block, BF16),
        ]
        + [pltpu.VMEM((batches + 1,) + block, F32)] * 4
        + [pltpu.SemaphoreType.DMA((8,))],
        compiler_params=params(56),
        cost_estimate=pl.CostEstimate(flops=12_000_000_000, bytes_accessed=4_000_000, transcendentals=0),
        name="near",
    )(me.reshape(1), pair_source, pair_offset, live_pairs.reshape(1, batches), operators.transpose(1, 2, 0), own, twin, other)

    many = 3 * batches + devices * slots
    return pl.pallas_call(
        far_kernel,
        out_shape=jax.ShapeDtypeStruct((batches, width), F32),
        in_specs=[HBM] * 8,
        out_specs=HBM,
        scratch_shapes=[
            pltpu.SMEM(late_shape, I32),
            pltpu.VMEM((many,) + block, BF16),
            pltpu.VMEM(ops_shape, BF16),
            pltpu.VMEM((batches,) + block, F32),
            pltpu.VMEM(occupied.shape, I32),
            pltpu.VMEM((many + 1, 2 * pairs, LANES), BF16),
            pltpu.VMEM(((batches + 1) * pairs, LANES), F32),
            pltpu.VMEM((batches, width), F32),
            pltpu.SemaphoreType.DMA((8,)),
        ],
        compiler_params=params(56),
        name="far",
    )(late, own, twin, other, ops, sums, arrived, occupied)


def solution(mesh):
    spec = P(("key", "lvl"), None)
    return jax.shard_map(
        local,
        mesh=mesh,
        in_specs=(spec, P(), spec, spec, P(("key", "lvl")), P(), spec),
        out_specs=spec,
        check_vma=False,
    )
```

```python
import functools

import jax
import jax.numpy as jnp
from jax import lax
from jax.experimental import pallas as pl
from jax.experimental.pallas import tpu as pltpu
from jax.sharding import PartitionSpec as P

F32 = jnp.float32
BF16 = jnp.bfloat16
I32 = jnp.int32
VMEM = pl.BlockSpec(memory_space=pltpu.VMEM)
SMEM = pl.BlockSpec(memory_space=pltpu.SMEM)
HBM = pl.BlockSpec(memory_space=pltpu.HBM)
GROUP = 64
SLOTS = 16
FEW = 4
ITEMS = 32
LANES = 128
NT = (((1,), (1,)), ((), ()))


def params(mib):
    return pltpu.CompilerParams(vmem_limit_bytes=mib << 20)


def padded(n, m):
    return -(-n // m) * m


def pack_kernel(me, send, m_hbm, own_hbm, outgoing_hbm, m, ids, scr, own, outgoing, sems):
    batches, pairs = own.shape[0], own.shape[1]
    slots, devices = ids.shape
    rows = pltpu.make_async_copy(m_hbm, m, sems.at[0])
    lists = pltpu.make_async_copy(send.at[me[0]], ids, sems.at[1])
    rows.start()
    lists.start()
    rows.wait()
    for i in range(pairs):
        for h in range(0, batches, 16):
            x = m[h : h + 16, i * LANES : (i + 1) * LANES].astype(F32)
            scr[pl.ds(h * pairs + i, 16, stride=pairs), :] = x
    for b in range(batches):
        own[b] = scr[b * pairs : (b + 1) * pairs, :].astype(BF16)
    keep = pltpu.make_async_copy(own, own_hbm, sems.at[2])
    keep.start()
    lists.wait()
    first = me[0] * batches
    part = devices // 4
    done = []
    for c in range(4):

        def send_to(j, _):
            for k in range(slots):
                outgoing[j * slots + k] = own[ids[k, j] - first]
            return 0

        lax.fori_loop(c * part, (c + 1) * part, send_to, 0, unroll=8)
        here = pl.ds(c * part * slots, part * slots)
        done.append(pltpu.make_async_copy(outgoing.at[here], outgoing_hbm.at[here], sems.at[3 + c]))
        done[-1].start()
    keep.wait()
    for copy in done:
        copy.wait()


def turn_ops(native, ops):
    coeffs, offsets = native.shape[0], native.shape[2]
    half = coeffs // 2
    tall = ops.shape[0]
    at = lax.broadcasted_iota(I32, (tall, offsets), 0)
    eye = jnp.where(at == lax.broadcasted_iota(I32, (tall, offsets), 1), 1.0, 0.0).astype(BF16)
    for i in range(0, half, 16):
        blocks = []
        for c in range(i, i + 16, 8):
            found = []
            for k in range(c, c + 8, 2):
                x = jnp.concatenate([native[k], native[half + k], native[k + 1], native[half + k + 1]], axis=0)
                y = lax.dot_general(eye, x, NT, preferred_element_type=F32)
                found += [y[:, :LANES], y[:, LANES:]]
            blocks.append(jnp.swapaxes(jnp.stack(found, axis=0), 0, 1))
        ops[:, i : i + 16, :] = jnp.concatenate(blocks, axis=1).astype(BF16)


def swapped(x):
    half = x.shape[1] // 2
    return jnp.concatenate([x[:, half:], x[:, :half]], axis=1)


def one_hot(want, row):
    return jnp.where(want == row, 1.0, 0.0).astype(BF16)


def make_tables(total_batches, me, src, off, live, near_slots, late):
    rows, lst = src.shape
    slots, wide = SLOTS, near_slots.shape[0]
    s = src[...]
    o = off[...]
    mine = me[0] * rows
    twin = (me[0] ^ 1) * rows
    other = (me[0] - 1 + 2 * (me[0] & 1)) * rows
    at_r = lax.broadcasted_iota(I32, (rows, rows), 0)
    at_c = lax.broadcasted_iota(I32, (rows, rows), 1)
    count_col = jnp.sum(jnp.where(at_r == at_c, live[...], 0), axis=1, keepdims=True)
    alive = lax.broadcasted_iota(I32, (rows, lst), 1) < count_col
    far = s >= total_batches
    in_mine = (s >= mine) & (s < mine + rows)
    in_twin = (s >= twin) & (s < twin + rows)
    place = jnp.where(in_mine, s - mine, jnp.where(in_twin, s - twin + rows, s - other + 2 * rows))
    place = jnp.where(far, s - total_batches + 3 * rows, place)
    value = jnp.where(alive, place + 1, 0)
    both = jnp.concatenate([value & 127, value >> 7], axis=0).astype(F32).astype(BF16)
    want = lax.broadcasted_iota(I32, (wide, lst), 0)
    lows, highs = [], []
    for t in range(rows):
        got = lax.dot_general(both, one_hot(want, o[t : t + 1, :]), NT, preferred_element_type=F32)
        lows.append(got[t : t + 1, :])
        highs.append(got[rows + t : rows + t + 1, :])
    low = jnp.concatenate(lows, axis=0)
    high = jnp.concatenate(highs, axis=0)
    value = (low + 128.0 * high).astype(I32)
    near = (value > 0) & (value <= 3 * rows)
    sooner = jnp.where(at_c < at_r, 1.0, 0.0).astype(BF16)
    rank = jnp.dot(sooner, jnp.where(near, 1.0, 0.0).astype(BF16), preferred_element_type=F32).astype(I32)
    target = lax.broadcasted_iota(I32, (rows, wide), 0)
    sources, targets = [], []
    for r in range(slots):
        sel = near & (rank == r)
        sources.append(jnp.sum(jnp.where(sel, value, 0), axis=0, keepdims=True))
        targets.append(jnp.sum(jnp.where(sel, target - rows, 0), axis=0, keepdims=True) + rows)
    table = jnp.concatenate(sources + targets, axis=0).astype(F32)
    near_slots[:, 0 : 2 * slots] = table.T.astype(I32)
    behind = (value > 3 * rows) | (near & (rank >= slots))
    one = jnp.where(behind, 1.0, 0.0)
    before = lax.broadcasted_iota(I32, (wide, wide), 0) < lax.broadcasted_iota(I32, (wide, wide), 1)
    order = jnp.dot(one.astype(BF16), jnp.where(before, 1.0, 0.0).astype(BF16), preferred_element_type=F32)
    pos = jnp.where(behind, order.astype(I32), wide)
    count = jnp.sum(one, axis=1, keepdims=True).astype(I32)
    items = jnp.maximum((count + (FEW - 1)) // FEW, 1)
    late[:, 0:wide] = jnp.zeros((late.shape[0], wide), I32)
    late[:, wide:] = jnp.ones((late.shape[0], late.shape[1] - wide), I32)
    late[0:rows, wide:] = jnp.broadcast_to(items, (rows, late.shape[1] - wide))
    want = lax.broadcasted_iota(I32, (wide, wide), 0)
    offset = lax.broadcasted_iota(I32, (16, wide), 1).astype(F32)
    parts = jnp.concatenate([low, high, offset], axis=0).astype(BF16)
    for t in range(rows):
        got = lax.dot_general(parts, one_hot(want, pos[t : t + 1, :]), NT, preferred_element_type=F32).astype(I32)
        source = got[t : t + 1, :] + 128 * got[rows + t : rows + t + 1, :]
        late[t : t + 1, 0:wide] = source * 256 + got[2 * rows : 2 * rows + 1, :]


def near_kernel(
    total_batches, me, src_hbm, off_hbm, live_hbm, native_hbm, own, twin, other,
    sums, ops_hbm, late_hbm,
    src, off, live, native, ops, late, slots_v, slot_t, pool, acc_a, acc_b, acc_c, acc_d, sems,
):
    batches, pairs = own.shape[0], own.shape[1]
    lists = []
    for n, (x, y) in enumerate(((src_hbm, src), (off_hbm, off), (live_hbm, live))):
        lists.append(pltpu.make_async_copy(x, y, sems.at[n]))
    fetch = pltpu.make_async_copy(native_hbm, native, sems.at[3])
    parts = []
    for n, part in enumerate((own, twin, other)):
        parts.append(pltpu.make_async_copy(part, pool.at[pl.ds(1 + n * batches, batches)], sems.at[4 + n]))
    for copy in lists + [fetch] + parts:
        copy.start()
    pool[0] = jnp.zeros(pool.shape[1:], BF16)
    accs = (acc_a, acc_b, acc_c, acc_d)
    for acc in accs:
        acc[...] = jnp.zeros_like(acc)
    for copy in lists:
        copy.wait()
    make_tables(total_batches, me, src, off, live, slots_v, late)
    to_smem = pltpu.make_async_copy(slots_v, slot_t, sems.at[7])
    to_smem.start()
    keep_late = pltpu.make_async_copy(late, late_hbm, sems.at[0])
    keep_late.start()
    fetch.wait()
    turn_ops(native, ops)
    keep = pltpu.make_async_copy(ops, ops_hbm, sems.at[1])
    keep.start()
    for copy in parts:
        copy.wait()
    to_smem.wait()
    slots = SLOTS
    blank = jnp.zeros(ops.shape[1:], BF16)
    none = jnp.zeros((LANES, LANES), BF16)
    low = lax.broadcasted_iota(I32, blank.shape, 1) < LANES // 2

    def twice(l):
        x = ops[l]
        y = swapped(x)
        first = [jnp.where(low, x, blank), jnp.where(low, y, blank)]
        return jnp.concatenate(first + [jnp.where(low, blank, y), jnp.where(low, blank, x)], axis=0)

    def group(g, _):
        for h in range(0, GROUP, 2):
            l = g * GROUP + h
            top = jnp.concatenate([twice(l), none], axis=1)
            end = jnp.concatenate([none, twice(l + 1)], axis=1)
            w = jnp.concatenate([top, end], axis=0)
            rows = [jnp.concatenate([pool[slot_t[l, r]], pool[slot_t[l + 1, r]]], axis=1) for r in range(slots)]
            y = lax.dot_general(jnp.concatenate(rows, axis=0), w, NT, preferred_element_type=F32)
            for side in range(2):
                acc = accs[(h % 4) // 2 * 2 + side]
                for r in range(0, slots, 4):
                    ats = [slot_t[l + side, slots + r + k] for k in range(4)]
                    olds = [acc[at] for at in ats]
                    for k in range(4):
                        new = y[(r + k) * pairs : (r + k + 1) * pairs, side * LANES : (side + 1) * LANES]
                        acc[ats[k]] = olds[k] + new
        return 0

    lax.fori_loop(0, slot_t.shape[0] // GROUP, group, 0)

    part = batches // 4
    done = []
    for c in range(4):
        for t in range(c * part, (c + 1) * part):
            acc_a[t] = (acc_a[t] + acc_b[t]) + (acc_c[t] + acc_d[t])
        here = pl.ds(c * part, part)
        done.append(pltpu.make_async_copy(acc_a.at[here], sums.at[here], sems.at[2 + c]))
        done[-1].start()
    keep_late.wait()
    keep.wait()
    for copy in done:
        copy.wait()


def far_kernel(
    table_hbm, own, twin, other, ops_hbm, near_hbm, arrived_hbm, occ_hbm, out_hbm,
    table, blocks, ops, near, occ, pool, acc, out, sems,
):
    batches, pairs = near.shape[0], near.shape[1]
    many = arrived_hbm.shape[0]
    last = table.shape[1] - 1
    fetch_table = pltpu.make_async_copy(table_hbm, table, sems.at[0])
    fetch_ops = pltpu.make_async_copy(ops_hbm, ops, sems.at[1])
    fetch_near = pltpu.make_async_copy(near_hbm, near, sems.at[2])
    fetch_occ = pltpu.make_async_copy(occ_hbm, occ, sems.at[3])
    parts = []
    for n, part in enumerate((own, twin, other, arrived_hbm)):
        here = pl.ds(n * batches, part.shape[0])
        parts.append(pltpu.make_async_copy(part, blocks.at[here], sems.at[4 + n]))
    for copy in [fetch_table] + parts + [fetch_ops, fetch_near, fetch_occ]:
        copy.start()
    acc[...] = jnp.zeros_like(acc)
    pool[0] = jnp.zeros(pool.shape[1:], BF16)

    def put(n, _):
        x = blocks[n]
        pool[1 + n, 0:pairs] = x
        pool[1 + n, pairs : 2 * pairs] = swapped(x)
        return 0

    for n, copy in enumerate(parts):
        copy.wait()
        lax.fori_loop(n * batches, n * batches + (batches if n < 3 else many), put, 0, unroll=16)
    fetch_table.wait()
    fetch_ops.wait()
    half = LANES // 2
    low = lax.broadcasted_iota(I32, (pairs, LANES), 1) < half
    total = lax.fori_loop(0, batches, lambda t, n: n + table[t, last], 0)

    def step(i, place):
        t, g = place
        for u in range(ITEMS):
            xs, ws = [], []
            for h in range(0, FEW, 2):
                e = g * FEW + h
                va, vb = table[t, e], table[t, e + 1]
                a, b = va >> 8, vb >> 8
                even = jnp.where(low, pool[a, 0:pairs], pool[b, pairs : 2 * pairs])
                odd = jnp.where(low, pool[a, pairs : 2 * pairs], pool[b, 0:pairs])
                xs.append(jnp.concatenate([even, odd], axis=0))
                wa, wb = ops[va & 255], ops[vb & 255]
                ws.append(jnp.concatenate([jnp.where(low, wa, swapped(wb)), jnp.where(low, swapped(wa), wb)], axis=0))
            r = lax.dot_general(jnp.concatenate(xs, axis=1), jnp.concatenate(ws, axis=1), NT, preferred_element_type=F32)
            at = pl.ds(pl.multiple_of(t * pairs, pairs), pairs)
            acc[at, :] += jnp.concatenate([r[:pairs], r[pairs:]], axis=1)
            end = g + 1 >= table[t, last]
            t = jnp.where(end, jnp.minimum(t + 1, batches), t)
            g = jnp.where(end, 0, g + 1)
        return t, g

    lax.fori_loop(0, (total + (ITEMS - 1)) // ITEMS, step, (jnp.int32(0), jnp.int32(0)))
    fetch_near.wait()
    fetch_occ.wait()

    def join(t, _):
        at = pl.ds(pl.multiple_of(t * pairs, pairs), pairs)
        acc[at, :] += near[t]
        return 0

    lax.fori_loop(0, batches, join, 0, unroll=8)
    cells = occ.shape[1]
    filled = occ[...].astype(F32).astype(BF16)
    cell = lax.broadcasted_iota(I32, (cells, LANES), 0)
    odd_cell = (lax.broadcasted_iota(I32, (cells, LANES), 1) >= half).astype(I32)
    done = []
    for i in range(pairs):
        spread = jnp.where(cell == odd_cell + 2 * i, 1.0, 0.0).astype(BF16)
        keep = jnp.dot(filled, spread, preferred_element_type=F32)
        out[:, i * LANES : (i + 1) * LANES] = acc[pl.ds(i, batches, stride=pairs), :] * keep
        if i % 8 == 7:
            here = pl.ds((i - 7) * LANES, 8 * LANES)
            done.append(pltpu.make_async_copy(out.at[:, here], out_hbm.at[:, here], sems.at[i // 8]))
            done[-1].start()
    for copy in done:
        copy.wait()


def local(multipoles, operators, pair_source, pair_offset, live_pairs, send_lists, occupied):
    axes = ("key", "lvl")
    batches, width = multipoles.shape
    offsets, coeffs = operators.shape[0], operators.shape[1]
    devices = lax.axis_size(axes)
    slots = send_lists.shape[2]
    me = lax.axis_index(axes)
    pairs = width // LANES
    wide = padded(offsets, GROUP)
    wide = padded(wide, 64)
    block = (pairs, LANES)

    own, outgoing = pl.pallas_call(
        pack_kernel,
        out_shape=(
            jax.ShapeDtypeStruct((batches,) + block, BF16),
            jax.ShapeDtypeStruct((devices * slots,) + block, BF16),
        ),
        in_specs=[SMEM, HBM, HBM],
        out_specs=(HBM, HBM),
        scratch_shapes=[
            pltpu.VMEM((batches, width), BF16),
            pltpu.SMEM((slots, devices), I32),
            pltpu.VMEM((batches * pairs, LANES), F32),
            pltpu.VMEM((batches,) + block, BF16),
            pltpu.VMEM((devices * slots,) + block, BF16),
            pltpu.SemaphoreType.DMA((7,)),
        ],
        compiler_params=params(56),
        name="pack",
    )(me.reshape(1), send_lists.transpose(0, 2, 1), multipoles)
    even = [(i, i ^ 1) for i in range(devices)]
    odd = [p for i in range(1, devices - 1, 2) for p in ((i, i + 1), (i + 1, i))]
    arrived = lax.all_to_all(outgoing, axes, split_axis=0, concat_axis=0, tiled=True)
    twin = lax.ppermute(own, axes, even)
    other = lax.ppermute(own, axes, odd)
    tall = padded(batches + 1, 8)
    ops_shape = (wide, coeffs // 2, LANES)
    late_shape = (tall, padded(wide + 1, LANES))
    sums, ops, late = pl.pallas_call(
        functools.partial(near_kernel, batches * devices),
        out_shape=(
            jax.ShapeDtypeStruct((batches,) + block, F32),
            jax.ShapeDtypeStruct(ops_shape, BF16),
            jax.ShapeDtypeStruct(late_shape, I32),
        ),
        in_specs=[SMEM] + [HBM] * 7,
        out_specs=(HBM,) * 3,
        scratch_shapes=[
            pltpu.VMEM((batches, offsets), I32),
            pltpu.VMEM((batches, offsets), I32),
            pltpu.VMEM((1, batches), I32),
            pltpu.VMEM((coeffs, coeffs, offsets), BF16),
            pltpu.VMEM(ops_shape, BF16),
            pltpu.VMEM(late_shape, I32),
            pltpu.VMEM((wide, LANES), I32),
            pltpu.SMEM((wide, LANES), I32),
            pltpu.VMEM((3 * batches + 1,) + block, BF16),
        ]
        + [pltpu.VMEM((batches + 1,) + block, F32)] * 4
        + [pltpu.SemaphoreType.DMA((8,))],
        compiler_params=params(56),
        cost_estimate=pl.CostEstimate(flops=12_000_000_000, bytes_accessed=4_000_000, transcendentals=0),
        name="near",
    )(me.reshape(1), pair_source, pair_offset, live_pairs.reshape(1, batches), operators.transpose(1, 2, 0), own, twin, other)

    many = 3 * batches + devices * slots
    return pl.pallas_call(
        far_kernel,
        out_shape=jax.ShapeDtypeStruct((batches, width), F32),
        in_specs=[HBM] * 8,
        out_specs=HBM,
        scratch_shapes=[
            pltpu.SMEM(late_shape, I32),
            pltpu.VMEM((many,) + block, BF16),
            pltpu.VMEM(ops_shape, BF16),
            pltpu.VMEM((batches,) + block, F32),
            pltpu.VMEM(occupied.shape, I32),
            pltpu.VMEM((many + 1, 2 * pairs, LANES), BF16),
            pltpu.VMEM(((batches + 1) * pairs, LANES), F32),
            pltpu.VMEM((batches, width), F32),
            pltpu.SemaphoreType.DMA((8,)),
        ],
        compiler_params=params(56),
        name="far",
    )(late, own, twin, other, ops, sums, arrived, occupied)


def solution(mesh):
    spec = P(("key", "lvl"), None)
    return jax.shard_map(
        local,
        mesh=mesh,
        in_specs=(spec, P(), spec, spec, P(("key", "lvl")), P(), spec),
        out_specs=spec,
        check_vma=False,
    )
```

```python
import functools

import jax
import jax.numpy as jnp
from jax import lax
from jax.experimental import pallas as pl
from jax.experimental.pallas import tpu as pltpu
from jax.sharding import PartitionSpec as P

F32 = jnp.float32
BF16 = jnp.bfloat16
I32 = jnp.int32
VMEM = pl.BlockSpec(memory_space=pltpu.VMEM)
SMEM = pl.BlockSpec(memory_space=pltpu.SMEM)
HBM = pl.BlockSpec(memory_space=pltpu.HBM)
GROUP = 64
SLOTS = 16
FEW = 4
ITEMS = 32
LANES = 128
NT = (((1,), (1,)), ((), ()))


def params(mib):
    return pltpu.CompilerParams(vmem_limit_bytes=mib << 20)


def padded(n, m):
    return -(-n // m) * m


def pack_kernel(me, send, m_hbm, own_hbm, outgoing_hbm, m, ids, scr, own, outgoing, sems):
    batches, pairs = own.shape[0], own.shape[1]
    slots, devices = ids.shape
    rows = pltpu.make_async_copy(m_hbm, m, sems.at[0])
    lists = pltpu.make_async_copy(send.at[me[0]], ids, sems.at[1])
    rows.start()
    lists.start()
    rows.wait()
    for i in range(pairs):
        for h in range(0, batches, 16):
            x = m[h : h + 16, i * LANES : (i + 1) * LANES].astype(F32)
            scr[pl.ds(h * pairs + i, 16, stride=pairs), :] = x
    for b in range(batches):
        own[b] = scr[b * pairs : (b + 1) * pairs, :].astype(BF16)
    keep = pltpu.make_async_copy(own, own_hbm, sems.at[2])
    keep.start()
    lists.wait()
    first = me[0] * batches
    part = devices // 4
    done = []
    for c in range(4):

        def send_to(j, _):
            for k in range(slots):
                outgoing[j * slots + k] = own[ids[k, j] - first]
            return 0

        lax.fori_loop(c * part, (c + 1) * part, send_to, 0, unroll=8)
        here = pl.ds(c * part * slots, part * slots)
        done.append(pltpu.make_async_copy(outgoing.at[here], outgoing_hbm.at[here], sems.at[3 + c]))
        done[-1].start()
    keep.wait()
    for copy in done:
        copy.wait()


def turn_ops(native, ops):
    coeffs, offsets = native.shape[0], native.shape[2]
    half = coeffs // 2
    tall = ops.shape[0]
    at = lax.broadcasted_iota(I32, (tall, offsets), 0)
    eye = jnp.where(at == lax.broadcasted_iota(I32, (tall, offsets), 1), 1.0, 0.0).astype(BF16)
    for i in range(0, half, 16):
        blocks = []
        for c in range(i, i + 16, 8):
            found = []
            for k in range(c, c + 8, 2):
                x = jnp.concatenate([native[k], native[half + k], native[k + 1], native[half + k + 1]], axis=0)
                y = lax.dot_general(eye, x, NT, preferred_element_type=F32)
                found += [y[:, :LANES], y[:, LANES:]]
            blocks.append(jnp.swapaxes(jnp.stack(found, axis=0), 0, 1))
        ops[:, i : i + 16, :] = jnp.concatenate(blocks, axis=1).astype(BF16)


def swapped(x):
    half = x.shape[1] // 2
    return jnp.concatenate([x[:, half:], x[:, :half]], axis=1)


def one_hot(want, row):
    return jnp.where(want == row, 1.0, 0.0).astype(BF16)


def make_tables(total_batches, me, src, off, live, near_slots, late):
    rows, lst = src.shape
    slots, wide = SLOTS, near_slots.shape[0]
    s = src[...]
    o = off[...]
    mine = me[0] * rows
    twin = (me[0] ^ 1) * rows
    other = (me[0] - 1 + 2 * (me[0] & 1)) * rows
    at_r = lax.broadcasted_iota(I32, (rows, rows), 0)
    at_c = lax.broadcasted_iota(I32, (rows, rows), 1)
    count_col = jnp.sum(jnp.where(at_r == at_c, live[...], 0), axis=1, keepdims=True)
    alive = lax.broadcasted_iota(I32, (rows, lst), 1) < count_col
    far = s >= total_batches
    in_mine = (s >= mine) & (s < mine + rows)
    in_twin = (s >= twin) & (s < twin + rows)
    place = jnp.where(in_mine, s - mine, jnp.where(in_twin, s - twin + rows, s - other + 2 * rows))
    place = jnp.where(far, s - total_batches + 3 * rows, place)
    value = jnp.where(alive, place + 1, 0)
    both = jnp.concatenate([value & 127, value >> 7], axis=0).astype(F32).astype(BF16)
    want = lax.broadcasted_iota(I32, (wide, lst), 0)
    lows, highs = [], []
    for t in range(rows):
        got = lax.dot_general(both, one_hot(want, o[t : t + 1, :]), NT, preferred_element_type=F32)
        lows.append(got[t : t + 1, :])
        highs.append(got[rows + t : rows + t + 1, :])
    low = jnp.concatenate(lows, axis=0)
    high = jnp.concatenate(highs, axis=0)
    value = (low + 128.0 * high).astype(I32)
    near = (value > 0) & (value <= 3 * rows)
    sooner = jnp.where(at_c < at_r, 1.0, 0.0).astype(BF16)
    rank = jnp.dot(sooner, jnp.where(near, 1.0, 0.0).astype(BF16), preferred_element_type=F32).astype(I32)
    target = lax.broadcasted_iota(I32, (rows, wide), 0)
    sources, targets = [], []
    for r in range(slots):
        sel = near & (rank == r)
        sources.append(jnp.sum(jnp.where(sel, value, 0), axis=0, keepdims=True))
        targets.append(jnp.sum(jnp.where(sel, target - rows, 0), axis=0, keepdims=True) + rows)
    table = jnp.concatenate(sources + targets, axis=0).astype(F32)
    near_slots[:, 0 : 2 * slots] = table.T.astype(I32)
    behind = (value > 3 * rows) | (near & (rank >= slots))
    one = jnp.where(behind, 1.0, 0.0)
    before = lax.broadcasted_iota(I32, (wide, wide), 0) < lax.broadcasted_iota(I32, (wide, wide), 1)
    order = jnp.dot(one.astype(BF16), jnp.where(before, 1.0, 0.0).astype(BF16), preferred_element_type=F32)
    pos = jnp.where(behind, order.astype(I32), wide)
    count = jnp.sum(one, axis=1, keepdims=True).astype(I32)
    items = jnp.maximum((count + (FEW - 1)) // FEW, 1)
    late[:, 0:wide] = jnp.zeros((late.shape[0], wide), I32)
    late[:, wide:] = jnp.ones((late.shape[0], late.shape[1] - wide), I32)
    late[0:rows, wide:] = jnp.broadcast_to(items, (rows, late.shape[1] - wide))
    want = lax.broadcasted_iota(I32, (wide, wide), 0)
    offset = lax.broadcasted_iota(I32, (16, wide), 1).astype(F32)
    parts = jnp.concatenate([low, high, offset], axis=0).astype(BF16)
    for t in range(rows):
        got = lax.dot_general(parts, one_hot(want, pos[t : t + 1, :]), NT, preferred_element_type=F32).astype(I32)
        source = got[t : t + 1, :] + 128 * got[rows + t : rows + t + 1, :]
        late[t : t + 1, 0:wide] = source * 256 + got[2 * rows : 2 * rows + 1, :]


def near_kernel(
    total_batches, me, src_hbm, off_hbm, live_hbm, native_hbm, own, twin, other,
    sums, ops_hbm, late_hbm,
    src, off, live, native, ops, late, slots_v, slot_t, pool, acc_a, acc_b, acc_c, acc_d, sems,
):
    batches, pairs = own.shape[0], own.shape[1]
    lists = []
    for n, (x, y) in enumerate(((src_hbm, src), (off_hbm, off), (live_hbm, live))):
        lists.append(pltpu.make_async_copy(x, y, sems.at[n]))
    fetch = pltpu.make_async_copy(native_hbm, native, sems.at[3])
    parts = []
    for n, part in enumerate((own, twin, other)):
        parts.append(pltpu.make_async_copy(part, pool.at[pl.ds(1 + n * batches, batches)], sems.at[4 + n]))
    for copy in lists + [fetch] + parts:
        copy.start()
    pool[0] = jnp.zeros(pool.shape[1:], BF16)
    accs = (acc_a, acc_b, acc_c, acc_d)
    for acc in accs:
        acc[...] = jnp.zeros_like(acc)
    for copy in lists:
        copy.wait()
    make_tables(total_batches, me, src, off, live, slots_v, late)
    to_smem = pltpu.make_async_copy(slots_v, slot_t, sems.at[7])
    to_smem.start()
    keep_late = pltpu.make_async_copy(late, late_hbm, sems.at[0])
    keep_late.start()
    fetch.wait()
    turn_ops(native, ops)
    keep = pltpu.make_async_copy(ops, ops_hbm, sems.at[1])
    keep.start()
    for copy in parts:
        copy.wait()
    to_smem.wait()
    slots = SLOTS
    blank = jnp.zeros(ops.shape[1:], BF16)
    none = jnp.zeros((LANES, LANES), BF16)
    low = lax.broadcasted_iota(I32, blank.shape, 1) < LANES // 2

    def twice(l):
        x = ops[l]
        y = swapped(x)
        first = [jnp.where(low, x, blank), jnp.where(low, y, blank)]
        return jnp.concatenate(first + [jnp.where(low, blank, y), jnp.where(low, blank, x)], axis=0)

    def group(g, _):
        for h in range(0, GROUP, 2):
            l = g * GROUP + h
            top = jnp.concatenate([twice(l), none], axis=1)
            end = jnp.concatenate([none, twice(l + 1)], axis=1)
            w = jnp.concatenate([top, end], axis=0)
            rows = [jnp.concatenate([pool[slot_t[l, r]], pool[slot_t[l + 1, r]]], axis=1) for r in range(slots)]
            y = lax.dot_general(jnp.concatenate(rows, axis=0), w, NT, preferred_element_type=F32)
            for side in range(2):
                acc = accs[(h % 4) // 2 * 2 + side]
                for r in range(0, slots, 2):
                    ats = [slot_t[l + side, slots + r + k] for k in range(2)]
                    olds = [acc[at] for at in ats]
                    for k in range(2):
                        new = y[(r + k) * pairs : (r + k + 1) * pairs, side * LANES : (side + 1) * LANES]
                        acc[ats[k]] = olds[k] + new
        return 0

    lax.fori_loop(0, slot_t.shape[0] // GROUP, group, 0)

    part = batches // 4
    done = []
    for c in range(4):
        for t in range(c * part, (c + 1) * part):
            acc_a[t] = (acc_a[t] + acc_b[t]) + (acc_c[t] + acc_d[t])
        here = pl.ds(c * part, part)
        done.append(pltpu.make_async_copy(acc_a.at[here], sums.at[here], sems.at[2 + c]))
        done[-1].start()
    keep_late.wait()
    keep.wait()
    for copy in done:
        copy.wait()


def far_kernel(
    table_hbm, own, twin, other, ops_hbm, near_hbm, arrived_hbm, occ_hbm, out_hbm,
    table, blocks, ops, near, occ, pool, acc, out, sems,
):
    batches, pairs = near.shape[0], near.shape[1]
    many = arrived_hbm.shape[0]
    last = table.shape[1] - 1
    fetch_table = pltpu.make_async_copy(table_hbm, table, sems.at[0])
    fetch_ops = pltpu.make_async_copy(ops_hbm, ops, sems.at[1])
    fetch_near = pltpu.make_async_copy(near_hbm, near, sems.at[2])
    fetch_occ = pltpu.make_async_copy(occ_hbm, occ, sems.at[3])
    parts = []
    for n, part in enumerate((own, twin, other, arrived_hbm)):
        here = pl.ds(n * batches, part.shape[0])
        parts.append(pltpu.make_async_copy(part, blocks.at[here], sems.at[4 + n]))
    for copy in [fetch_table] + parts + [fetch_ops, fetch_near, fetch_occ]:
        copy.start()
    acc[...] = jnp.zeros_like(acc)
    pool[0] = jnp.zeros(pool.shape[1:], BF16)

    def put(n, _):
        x = blocks[n]
        pool[1 + n, 0:pairs] = x
        pool[1 + n, pairs : 2 * pairs] = swapped(x)
        return 0

    for n, copy in enumerate(parts):
        copy.wait()
        lax.fori_loop(n * batches, n * batches + (batches if n < 3 else many), put, 0, unroll=16)
    fetch_table.wait()
    fetch_ops.wait()
    half = LANES // 2
    low = lax.broadcasted_iota(I32, (pairs, LANES), 1) < half
    total = lax.fori_loop(0, batches, lambda t, n: n + table[t, last], 0)

    def step(i, place):
        t, g = place
        for u in range(ITEMS):
            xs, ws = [], []
            for h in range(0, FEW, 2):
                e = g * FEW + h
                va, vb = table[t, e], table[t, e + 1]
                a, b = va >> 8, vb >> 8
                even = jnp.where(low, pool[a, 0:pairs], pool[b, pairs : 2 * pairs])
                odd = jnp.where(low, pool[a, pairs : 2 * pairs], pool[b, 0:pairs])
                xs.append(jnp.concatenate([even, odd], axis=0))
                wa, wb = ops[va & 255], ops[vb & 255]
                ws.append(jnp.concatenate([jnp.where(low, wa, swapped(wb)), jnp.where(low, swapped(wa), wb)], axis=0))
            r = lax.dot_general(jnp.concatenate(xs, axis=1), jnp.concatenate(ws, axis=1), NT, preferred_element_type=F32)
            at = pl.ds(pl.multiple_of(t * pairs, pairs), pairs)
            acc[at, :] += jnp.concatenate([r[:pairs], r[pairs:]], axis=1)
            end = g + 1 >= table[t, last]
            t = jnp.where(end, jnp.minimum(t + 1, batches), t)
            g = jnp.where(end, 0, g + 1)
        return t, g

    lax.fori_loop(0, (total + (ITEMS - 1)) // ITEMS, step, (jnp.int32(0), jnp.int32(0)))
    fetch_near.wait()
    fetch_occ.wait()

    def join(t, _):
        at = pl.ds(pl.multiple_of(t * pairs, pairs), pairs)
        acc[at, :] += near[t]
        return 0

    lax.fori_loop(0, batches, join, 0, unroll=8)
    cells = occ.shape[1]
    filled = occ[...].astype(F32).astype(BF16)
    cell = lax.broadcasted_iota(I32, (cells, LANES), 0)
    odd_cell = (lax.broadcasted_iota(I32, (cells, LANES), 1) >= half).astype(I32)
    done = []
    for i in range(pairs):
        spread = jnp.where(cell == odd_cell + 2 * i, 1.0, 0.0).astype(BF16)
        keep = jnp.dot(filled, spread, preferred_element_type=F32)
        out[:, i * LANES : (i + 1) * LANES] = acc[pl.ds(i, batches, stride=pairs), :] * keep
        if i % 8 == 7:
            here = pl.ds((i - 7) * LANES, 8 * LANES)
            done.append(pltpu.make_async_copy(out.at[:, here], out_hbm.at[:, here], sems.at[i // 8]))
            done[-1].start()
    for copy in done:
        copy.wait()


def local(multipoles, operators, pair_source, pair_offset, live_pairs, send_lists, occupied):
    axes = ("key", "lvl")
    batches, width = multipoles.shape
    offsets, coeffs = operators.shape[0], operators.shape[1]
    devices = lax.axis_size(axes)
    slots = send_lists.shape[2]
    me = lax.axis_index(axes)
    pairs = width // LANES
    wide = padded(offsets, GROUP)
    wide = padded(wide, 64)
    block = (pairs, LANES)

    own, outgoing = pl.pallas_call(
        pack_kernel,
        out_shape=(
            jax.ShapeDtypeStruct((batches,) + block, BF16),
            jax.ShapeDtypeStruct((devices * slots,) + block, BF16),
        ),
        in_specs=[SMEM, HBM, HBM],
        out_specs=(HBM, HBM),
        scratch_shapes=[
            pltpu.VMEM((batches, width), BF16),
            pltpu.SMEM((slots, devices), I32),
            pltpu.VMEM((batches * pairs, LANES), F32),
            pltpu.VMEM((batches,) + block, BF16),
            pltpu.VMEM((devices * slots,) + block, BF16),
            pltpu.SemaphoreType.DMA((7,)),
        ],
        compiler_params=params(56),
        name="pack",
    )(me.reshape(1), send_lists.transpose(0, 2, 1), multipoles)
    even = [(i, i ^ 1) for i in range(devices)]
    odd = [p for i in range(1, devices - 1, 2) for p in ((i, i + 1), (i + 1, i))]
    arrived = lax.all_to_all(outgoing, axes, split_axis=0, concat_axis=0, tiled=True)
    twin = lax.ppermute(own, axes, even)
    other = lax.ppermute(own, axes, odd)
    tall = padded(batches + 1, 8)
    ops_shape = (wide, coeffs // 2, LANES)
    late_shape = (tall, padded(wide + 1, LANES))
    sums, ops, late = pl.pallas_call(
        functools.partial(near_kernel, batches * devices),
        out_shape=(
            jax.ShapeDtypeStruct((batches,) + block, F32),
            jax.ShapeDtypeStruct(ops_shape, BF16),
            jax.ShapeDtypeStruct(late_shape, I32),
        ),
        in_specs=[SMEM] + [HBM] * 7,
        out_specs=(HBM,) * 3,
        scratch_shapes=[
            pltpu.VMEM((batches, offsets), I32),
            pltpu.VMEM((batches, offsets), I32),
            pltpu.VMEM((1, batches), I32),
            pltpu.VMEM((coeffs, coeffs, offsets), BF16),
            pltpu.VMEM(ops_shape, BF16),
            pltpu.VMEM(late_shape, I32),
            pltpu.VMEM((wide, LANES), I32),
            pltpu.SMEM((wide, LANES), I32),
            pltpu.VMEM((3 * batches + 1,) + block, BF16),
        ]
        + [pltpu.VMEM((batches + 1,) + block, F32)] * 4
        + [pltpu.SemaphoreType.DMA((8,))],
        compiler_params=params(56),
        cost_estimate=pl.CostEstimate(flops=12_000_000_000, bytes_accessed=4_000_000, transcendentals=0),
        name="near",
    )(me.reshape(1), pair_source, pair_offset, live_pairs.reshape(1, batches), operators.transpose(1, 2, 0), own, twin, other)

    many = 3 * batches + devices * slots
    return pl.pallas_call(
        far_kernel,
        out_shape=jax.ShapeDtypeStruct((batches, width), F32),
        in_specs=[HBM] * 8,
        out_specs=HBM,
        scratch_shapes=[
            pltpu.SMEM(late_shape, I32),
            pltpu.VMEM((many,) + block, BF16),
            pltpu.VMEM(ops_shape, BF16),
            pltpu.VMEM((batches,) + block, F32),
            pltpu.VMEM(occupied.shape, I32),
            pltpu.VMEM((many + 1, 2 * pairs, LANES), BF16),
            pltpu.VMEM(((batches + 1) * pairs, LANES), F32),
            pltpu.VMEM((batches, width), F32),
            pltpu.SemaphoreType.DMA((8,)),
        ],
        compiler_params=params(56),
        name="far",
    )(late, own, twin, other, ops, sums, arrived, occupied)


def solution(mesh):
    spec = P(("key", "lvl"), None)
    return jax.shard_map(
        local,
        mesh=mesh,
        in_specs=(spec, P(), spec, spec, P(("key", "lvl")), P(), spec),
        out_specs=spec,
        check_vma=False,
    )
```
